512 devices in a mesh: tok: 128 (over z, x, core), hd: 4 (over y).
Axes of the slice: x: 4, y: 4, z: 16, core: 2. Of those that a mesh axis runs over, the one named last changes fastest.
Arguments:
- query: bfloat16 [16384, 8192], P('tok', 'hd'), may hold values from -6 to 6
- keys: bfloat16 [16384, 1024], P(('tok', 'hd')), may hold values from -6 to 6
- values: bfloat16 [16384, 1024], P(('tok', 'hd')), may hold values from -6 to 6
- grad_out: bfloat16 [16384, 8192], P('tok', 'hd'), may hold values from -6 to 6
- delta: float32 [16384, 64], P('tok', 'hd'), may hold values from -24 to 24
- segments: int32 [16384], replicated, may hold values from 0 to 127, never falling along the last dimension, each value on 1 to 512 neighbouring positions
Outputs:
- grad_query: bfloat16 [16384, 8192], P('tok', 'hd')
- grad_key: bfloat16 [16384, 1024], P(('tok', 'hd'))
- grad_value: bfloat16 [16384, 1024], P(('tok', 'hd'))
The draws below stay inside these ranges and needn't reach their ends.
Inputs may be any that keep to these rules, and one draw needn't show every extreme that they name: `segments`: ids never fall along the tokens; each document holds 1 to 512 tokens and one holds exactly 512.
All inputs are finite; a program needn't handle non-finite values.
Results may differ from the reference program's by a relative error of at most 0.0049.
Values may be sent and summed in bfloat16 or wider, within the bound.
A program may use at most 64 MiB of HBM per device.

```python
import math
import jax
import jax.numpy as jnp
import numpy as np
from jax import lax

QH = 64
KVH = 8
HD = 128
TOK_DEV = 128
WIN = 4
TOKENS = 16384
DOC_MOST = 512
DOCS = 128
N_TOK = 128


def draw_query(key, part):
    result = jnp.clip(jax.random.normal(jax.random.fold_in(key, 3), (TOKENS, QH * HD), jnp.float32), -6.0, 6.0)
    return result.astype(jnp.bfloat16)


def draw_keys(key, part):
    result = jnp.clip(jax.random.normal(jax.random.fold_in(key, 5), (TOKENS, KVH * HD), jnp.float32), -6.0, 6.0)
    return result.astype(jnp.bfloat16)


def steps_of(stream_key, extent, split, least, top_value):
    loudness, own = 1.0, jax.random.fold_in(stream_key, 6)
    for axis_at, blocks in split:
        draws = jnp.exp(jax.random.uniform(jax.random.fold_in(own, axis_at), (blocks,), jnp.float32, least / len(split), top_value / len(split)))
        loudness = loudness * jnp.repeat(draws, extent[axis_at] // blocks).reshape([-1 if axis == axis_at else 1 for axis in range(len(extent))])
    return loudness


def profile(number_of, total, bound, slope):
    weights = [(1 << 20) // math.isqrt(rank ** slope) + 1 for rank in range(2, number_of + 1)]
    spare, holding = total - bound - (number_of - 1), [1] * (number_of - 1)
    while spare > 0:
        movable = [i for i in range(number_of - 1) if holding[i] < bound]
        mass, budget = sum([weights[i] for i in movable]), spare
        for i in movable:
            addition = min(bound - holding[i], max(1, budget * weights[i] // mass), spare)
            holding[i] = holding[i] + addition
            spare = spare - addition
    return np.array([bound] + holding)


def ragged(own_key, amount, total, limit, skew):
    if amount == 2:
        one = jax.random.randint(own_key, (), max(1, total - limit), min(limit, total - 1) + 1)
        return jnp.stack([one, total - one])
    sizes = jnp.asarray(profile(amount, total, limit, skew), jnp.int32)
    twos = (amount - 1) // 2
    donor, sink = sizes[1:1 + 2 * twos:2], sizes[2:2 + 2 * twos:2]
    slack = jnp.minimum(donor - 1, limit - sink)
    moved = jax.random.randint(jax.random.fold_in(own_key, 1), (twos,), 0, 1 << 20) % (slack + 1)
    sizes = sizes.at[1:1 + 2 * twos:2].set(donor - moved).at[2:2 + 2 * twos:2].set(sink + moved)
    return sizes[jax.random.permutation(jax.random.fold_in(own_key, 2), amount)]


def bell_draw(stream_key, dims, scale, reach, pieces=(), held_as=jnp.bfloat16):
    drawn = jax.random.normal(stream_key, dims, jnp.float32) * scale
    if len(pieces) > 0:
        drawn = steps_of(stream_key, dims, pieces, -0.22, 0.18) * drawn
    return jnp.clip(drawn, min=-reach, max=reach).astype(held_as)


def setup_inputs(seed: int = 0) -> dict:
    arg_keys = jax.random.split(jax.random.key(seed), 7)
    return {
        "query": draw_query(jax.random.fold_in(arg_keys[6], 71), 0),
        "keys": draw_keys(jax.random.fold_in(arg_keys[6], 71), 0),
        "values": bell_draw(arg_keys[2], (TOKENS, KVH * HD), 1.0, 6.0, ((0, 512),)),
        "grad_out": bell_draw(arg_keys[3], (TOKENS, QH * HD), 1.0, 6.0, ((0, 128), (1, 4))),
        "delta": bell_draw(arg_keys[4], (TOKENS, QH), 4.0, 24.0, ((0, 128), (1, 4)), jnp.float32),
        "segments": jnp.searchsorted(jnp.cumsum(ragged(arg_keys[5], DOCS, TOKENS, DOC_MOST, 2)), jnp.arange(TOKENS), side="right").astype(jnp.int32),
    }


NEG_FILL = -1e+30

def reference(query, keys, values, grad_out, delta, segments):
    heads = delta.shape[1]
    width = query.shape[1] // heads
    groups = keys.shape[1] // width
    repeat = heads // groups
    scale_factor = 1.0 / math.sqrt(width)
    lead_rows = WIN * TOK_DEV
    span_rows = lead_rows + TOK_DEV
    key_pad = jnp.concatenate([jnp.zeros((lead_rows, keys.shape[1]), keys.dtype), keys], 0)
    value_pad = jnp.concatenate([jnp.zeros((lead_rows, values.shape[1]), values.dtype), values], 0)
    seg_pad = jnp.concatenate([jnp.full((lead_rows,), -1, jnp.int32), segments.astype(jnp.int32)])
    query_blocks = query.reshape(N_TOK, TOK_DEV, groups, repeat, width)
    grad_blocks = grad_out.reshape(N_TOK, TOK_DEV, groups, repeat, width)
    delta_blocks = delta.reshape(N_TOK, TOK_DEV, groups, repeat)
    causal = jnp.arange(span_rows)[None, :] <= jnp.arange(TOK_DEV)[:, None] + lead_rows

    def one_block(accums, inputs):
        accum_key, accum_value = accums
        query_blk, grad_blk, delta_blk, block_index = inputs
        row_start = (block_index * TOK_DEV).astype(jnp.int32)
        key_rows = lax.dynamic_slice_in_dim(key_pad, row_start, span_rows, 0).reshape(span_rows, groups, width).astype(jnp.float32)
        value_rows = lax.dynamic_slice_in_dim(value_pad, row_start, span_rows, 0).reshape(span_rows, groups, width).astype(jnp.float32)
        key_seg = lax.dynamic_slice_in_dim(seg_pad, row_start, span_rows, 0)
        query_seg = lax.dynamic_slice_in_dim(segments.astype(jnp.int32), row_start, TOK_DEV, 0)
        allowed = (key_seg[None, :] == query_seg[:, None]) & causal
        query_full = query_blk.astype(jnp.float32)
        grad_full = grad_blk.astype(jnp.float32)
        scores = jnp.einsum('qgrd,kgd->grqk', query_full, key_rows) * scale_factor
        scores = jnp.where(allowed, scores, NEG_FILL)
        row_top = lax.optimization_barrier(jnp.max(scores, axis=-1, keepdims=True))
        row_sum = lax.optimization_barrier(jnp.sum(jnp.where(allowed, jnp.exp(scores - row_top), 0.0), axis=-1, keepdims=True))
        weights = jnp.where(allowed, jnp.exp(scores - row_top) / row_sum, 0.0)
        weights_low = lax.optimization_barrier(weights.astype(jnp.bfloat16)).astype(jnp.float32)
        grad_weights = jnp.einsum('qgrd,kgd->grqk', grad_full, value_rows)
        row_delta = jnp.transpose(delta_blk, (1, 2, 0))[..., None]
        grad_scores = weights * (grad_weights - row_delta)
        grad_scores = lax.optimization_barrier(grad_scores.astype(jnp.bfloat16)).astype(jnp.float32)
        grad_query = jnp.einsum('grqk,kgd->qgrd', grad_scores, key_rows) * scale_factor
        grad_key = jnp.einsum('grqk,qgrd->kgd', grad_scores, query_full) * scale_factor
        grad_value = jnp.einsum('grqk,qgrd->kgd', weights_low, grad_full)
        old_key = lax.dynamic_slice_in_dim(accum_key, row_start, span_rows, 0)
        old_value = lax.dynamic_slice_in_dim(accum_value, row_start, span_rows, 0)
        accum_key = lax.dynamic_update_slice_in_dim(accum_key, old_key + grad_key.reshape(span_rows, groups * width), row_start, 0)
        accum_value = lax.dynamic_update_slice_in_dim(accum_value, old_value + grad_value.reshape(span_rows, groups * width), row_start, 0)
        return ((accum_key, accum_value), grad_query.reshape(TOK_DEV, heads * width).astype(jnp.bfloat16))
    zero_grads = jnp.zeros((lead_rows + query.shape[0], groups * width), jnp.float32)
    (accum_key, accum_value), grad_query = lax.scan(one_block, (zero_grads, zero_grads), (query_blocks, grad_blocks, delta_blocks, jnp.arange(N_TOK, dtype=jnp.int32)))
    return (grad_query.reshape(query.shape[0], heads * width), accum_key[lead_rows:].astype(jnp.bfloat16), accum_value[lead_rows:].astype(jnp.bfloat16))
```

```python
import math

import jax
import jax.numpy as jnp
from jax import lax
from jax.experimental import pallas as pl
from jax.experimental.pallas import tpu as pltpu
from jax.sharding import PartitionSpec as P

MESH = pl.DeviceIdType.MESH
HD = 128
HEADS = 8
TOK = 128
PAIR = 2 * TOK
SPAN = 3 * PAIR
SEEN = 5 * TOK
HALF = HEADS * HD
PIECE = 32
FILL = -1e30
SCALE = 1.0 / math.sqrt(HD)
LOG2E = math.log2(math.e)
PARTNERS = [(0, 2), (1, 2), (0, 1), (0, 3), (1, 1), (1, 3), (1, 0)]
NT = (((1,), (1,)), ((), ()))


def aligned(index, size):
    return pl.multiple_of(index * size, size)


def kernel(
    query, keys, values, grad_out, delta, segments,
    dq_out, dk_out, dv_out,
    qb, gb, dt, sb, kb, vb, kt, scores, gweights, probs, dscores, bias,
    own, outbox, inbox, totals, dqs,
    local_sem, kv_send, kv_recv, pair_send, pair_recv,
    shift_send, shift_recv, back_send, back_recv, fin_send, fin_recv, dq_send, dq_recv,
):
    tok, hd = lax.axis_index("tok"), lax.axis_index("hd")
    chips = lax.axis_size("tok") // 2
    rows_y = lax.axis_size("hd")
    core, chip = lax.rem(tok, 2), lax.div(tok, 2)
    other = 1 - core

    def local(index, src, dst):
        copy = pltpu.make_async_copy(src, dst, local_sem.at[index])
        copy.start()
        return copy

    def remote(src, dst, send, recv, to_tok, to_hd):
        return pltpu.make_async_remote_copy(
            src_ref=src, dst_ref=dst, send_sem=send, recv_sem=recv,
            device_id=(to_tok, to_hd), device_id_type=MESH,
        )

    def partner(k):
        cross, step = PARTNERS[k]
        pcore = other if cross else core
        return pcore, lax.rem(hd + step, rows_y)

    mine = pl.ds(aligned(2 * hd + core, HD), HD)
    slot = pl.ds(pl.multiple_of((4 + core) * TOK + PIECE * hd, PIECE), PIECE)
    half = pl.ds(aligned(core, HALF), HALF)
    far_half = pl.ds(aligned(other, HALF), HALF)
    my_rows = pl.ds(aligned(core, TOK), TOK)
    loc_k = local(0, keys.at[:, mine], kb.at[slot])
    loc_v = local(1, values.at[:, mine], vb.at[slot])
    loc_s = local(2, segments, sb)

    barrier = pltpu.get_barrier_semaphore()
    for k in range(len(PARTNERS)):
        pcore, ph = partner(k)
        pl.semaphore_signal(barrier, 1, device_id=(2 * chip + pcore, ph), device_id_type=MESH)
    for step in (1, 2):
        @pl.when(chip + step < chips)
        def _(step=step):
            pl.semaphore_signal(barrier, 1, device_id=(tok + 2 * step, hd), device_id_type=MESH)

        @pl.when(chip >= step)
        def _(step=step):
            pl.semaphore_signal(barrier, 1, device_id=(tok - 2 * step, hd), device_id_type=MESH)

    near = sum(
        jnp.where(c, 1, 0)
        for c in (chip >= 1, chip >= 2, chip + 1 < chips, chip + 2 < chips)
    )
    pl.semaphore_wait(barrier, len(PARTNERS) + near)

    kv_copies = []
    for which, (source, target) in enumerate(((keys, kb), (values, vb))):
        for k in range(len(PARTNERS)):
            pcore, ph = partner(k)
            cols = pl.ds(aligned(2 * ph + pcore, HD), HD)
            copy = remote(
                source.at[:, cols], target.at[slot],
                kv_send.at[which, k], kv_recv.at[which, k], 2 * chip + pcore, ph,
            )
            copy.start()
            kv_copies.append(copy)
    pair_copies = []
    for k, (src, dst) in enumerate((
        (query.at[:, far_half], qb.at[my_rows]),
        (grad_out.at[:, far_half], gb.at[my_rows]),
        (delta, dt.at[core]),
    )):
        copy = remote(src, dst, pair_send.at[k], pair_recv.at[k], 2 * chip + other, hd)
        copy.start()
        pair_copies.append(copy)
    loc_q = local(3, query.at[:, half], qb.at[my_rows])
    loc_g = local(4, grad_out.at[:, half], gb.at[my_rows])
    loc_d = local(5, delta, dt.at[core])

    for step in (1, 2):
        @pl.when(chip < step)
        def _(step=step):
            empty = pl.ds((2 - step) * PAIR, PAIR)
            kb[empty, :] = jnp.zeros((PAIR, HD), kb.dtype)
            vb[empty, :] = jnp.zeros((PAIR, HD), vb.dtype)

        @pl.when(chip + step >= chips)
        def _(step=step):
            inbox[step - 1] = jnp.zeros(inbox.shape[1:], inbox.dtype)

    loc_s.wait()

    def ids(shard):
        row = sb[pl.ds(jnp.maximum(shard, 0), 1), :]
        return jnp.where(shard < 0, -1, row)

    shards = [2 * chip - 4 + s for s in range(6)]
    rows = [ids(s) for s in shards]
    tall = [jnp.transpose(jnp.broadcast_to(r, (TOK, TOK))) for r in rows]
    key_at = lax.broadcasted_iota(jnp.int32, (TOK, TOK), 0)
    query_at = lax.broadcasted_iota(jnp.int32, (TOK, TOK), 1)
    for b in range(2):
        for s in range(5):
            allowed = tall[b + s] == rows[4 + b]
            if s == 4:
                allowed = allowed & (key_at <= query_at)
            bias[b, s * TOK : (s + 1) * TOK, :] = jnp.where(allowed, 0.0, FILL)
    nothing = jnp.zeros((TOK, TOK), probs.dtype)
    for head in range(HEADS):
        for ref in (probs, dscores):
            ref[SEEN:SPAN, head * PAIR : head * PAIR + TOK] = nothing
            ref[0:TOK, head * PAIR + TOK : (head + 1) * PAIR] = nothing

    shift = [[[None] * 2 for _ in range(2)] for _ in range(2)]
    for which, (ref, loc) in enumerate(((kb, loc_k), (vb, loc_v))):
        loc.wait()
        for k in range(len(PARTNERS)):
            kv_copies[which * len(PARTNERS) + k].wait_recv()
        for step in (1, 2):
            copy = remote(
                ref.at[pl.ds(2 * PAIR, PAIR)], ref.at[pl.ds((2 - step) * PAIR, PAIR)],
                shift_send.at[step - 1, which], shift_recv.at[step - 1, which],
                tok + 2 * step, hd,
            )
            shift[step - 1][which] = copy

            @pl.when(chip + step < chips)
            def _(copy=copy):
                copy.start()

    loc_q.wait()
    loc_g.wait()
    loc_d.wait()
    for copy in pair_copies:
        copy.wait_recv()

    def products(block):
        span = slice(block * PAIR, (block + 1) * PAIR)

        def body(head, _):
            cols = pl.ds(aligned(head, HD), HD)
            scores[head, span, :] = lax.dot_general(
                kb[span, :], qb[:, cols], NT, preferred_element_type=jnp.float32
            )
            gweights[head, span, :] = lax.dot_general(
                vb[span, :], gb[:, cols], NT, preferred_element_type=jnp.float32
            )
            return 0

        lax.fori_loop(0, HEADS, body, 0)
        kt[:, span] = jnp.transpose(kb[span, :])

    products(2)
    for step in (1, 2):
        @pl.when(chip >= step)
        def _(step=step):
            for which in range(2):
                shift[step - 1][which].wait_recv()

        products(2 - step)

    def softmax(head, _):
        for b in range(2):
            span = slice(b * TOK, b * TOK + SEEN)
            lanes = slice(b * TOK, (b + 1) * TOK)
            raw = scores[head, span, lanes] + bias[b]
            top = jnp.max(raw, axis=0, keepdims=True)
            grown = jnp.exp2((raw - top) * (SCALE * LOG2E))
            total = jnp.sum(grown, axis=0, keepdims=True)
            weights = grown * (1.0 / total)
            row_delta = dt[b, pl.ds(core * HEADS + head, 1), :]
            grads = weights * (gweights[head, span, lanes] - row_delta)
            cols = pl.ds(pl.multiple_of(head * PAIR + b * TOK, TOK), TOK)
            probs[span, cols] = weights.astype(probs.dtype)
            dscores[span, cols] = grads.astype(dscores.dtype)
        return 0

    lax.fori_loop(0, HEADS, softmax, 0)

    def key_value_grads(block):
        span = slice(block * PAIR, (block + 1) * PAIR)
        dk = jnp.zeros((PAIR, HD), jnp.float32)
        dv = jnp.zeros((PAIR, HD), jnp.float32)
        for head in range(HEADS):
            lanes = slice(head * PAIR, (head + 1) * PAIR)
            cols = slice(head * HD, (head + 1) * HD)
            dk += jnp.dot(dscores[span, lanes], qb[:, cols], preferred_element_type=jnp.float32)
            dv += jnp.dot(probs[span, lanes], gb[:, cols], preferred_element_type=jnp.float32)
        return dk * SCALE, dv

    back = [None, None]
    for step in (2, 1):
        dk, dv = key_value_grads(2 - step)
        outbox[step - 1, 0] = dk.astype(outbox.dtype)
        outbox[step - 1, 1] = dv.astype(outbox.dtype)
        copy = remote(
            outbox.at[step - 1], inbox.at[step - 1],
            back_send.at[step - 1], back_recv.at[step - 1], tok - 2 * step, hd,
        )
        back[step - 1] = copy

        @pl.when(chip >= step)
        def _(copy=copy):
            copy.start()

    dk, dv = key_value_grads(2)
    own[0] = dk
    own[1] = dv

    def query_grads(head, _):
        lanes = pl.ds(aligned(head, PAIR), PAIR)
        turned = jnp.dot(kt[...], dscores[:, lanes], preferred_element_type=jnp.float32)
        turned = turned * SCALE
        cols = pl.ds(aligned(head, HD), HD)
        for b in range(2):
            block = jnp.transpose(turned[:, b * TOK : (b + 1) * TOK])
            dqs[b, :, cols] = block.astype(dqs.dtype)
        return 0

    lax.fori_loop(0, HEADS, query_grads, 0)
    dq_copy = remote(
        dqs.at[other], dq_out.at[:, half], dq_send.at[0], dq_recv.at[0], 2 * chip + other, hd
    )
    dq_copy.start()
    loc_dq = local(6, dqs.at[core], dq_out.at[:, half])

    for step in (1, 2):
        @pl.when(chip + step < chips)
        def _(step=step):
            back[step - 1].wait_recv()

    for which in range(2):
        total = own[which]
        for step in range(2):
            total += inbox[step, which].astype(jnp.float32)
        totals[which] = total.astype(totals.dtype)
    fin_copies = []
    for which, out in enumerate((dk_out, dv_out)):
        for k in range(len(PARTNERS)):
            pcore, ph = partner(k)
            src_rows = pl.ds(pl.multiple_of(pcore * TOK + PIECE * ph, PIECE), PIECE)
            copy = remote(
                totals.at[which, src_rows], out.at[:, mine],
                fin_send.at[which, k], fin_recv.at[which, k], 2 * chip + pcore, ph,
            )
            copy.start()
            fin_copies.append(copy)
    own_rows = pl.ds(pl.multiple_of(core * TOK + PIECE * hd, PIECE), PIECE)
    loc_dk = local(7, totals.at[0, own_rows], dk_out.at[:, mine])
    loc_dv = local(8, totals.at[1, own_rows], dv_out.at[:, mine])

    for copy in kv_copies + pair_copies:
        copy.wait_send()
    for step in (1, 2):
        @pl.when(chip + step < chips)
        def _(step=step):
            for which in range(2):
                shift[step - 1][which].wait_send()

        @pl.when(chip >= step)
        def _(step=step):
            back[step - 1].wait_send()

    loc_dq.wait()
    loc_dk.wait()
    loc_dv.wait()
    dq_copy.wait()
    for copy in fin_copies:
        copy.wait()


def on_device(query, keys, values, grad_out, delta, segments):
    low, full = jnp.bfloat16, jnp.float32
    tokens = query.shape[0]
    dma = pltpu.SemaphoreType.DMA
    partners = len(PARTNERS)
    return tuple(pl.pallas_call(
        kernel,
        out_shape=(
            pltpu.VMEM(query.shape, low),
            pltpu.VMEM(keys.shape, low),
            pltpu.VMEM(values.shape, low),
        ),
        in_specs=[pl.BlockSpec(memory_space=pl.ANY)] * 6,
        out_specs=[pl.BlockSpec(memory_space=pltpu.VMEM)] * 3,
        scratch_shapes=[
            pltpu.VMEM((PAIR, HALF), low),
            pltpu.VMEM((PAIR, HALF), low),
            pltpu.VMEM((2,) + delta.shape[::-1], full),
            pltpu.VMEM((segments.shape[0] // TOK, TOK), jnp.int32),
            pltpu.VMEM((SPAN, HD), low),
            pltpu.VMEM((SPAN, HD), low),
            pltpu.VMEM((HD, SPAN), low),
            pltpu.VMEM((HEADS, SPAN, PAIR), full),
            pltpu.VMEM((HEADS, SPAN, PAIR), full),
            pltpu.VMEM((SPAN, HEADS * PAIR), low),
            pltpu.VMEM((SPAN, HEADS * PAIR), low),
            pltpu.VMEM((2, SEEN, TOK), full),
            pltpu.VMEM((2, PAIR, HD), full),
            pltpu.VMEM((2, 2, PAIR, HD), low),
            pltpu.VMEM((2, 2, PAIR, HD), low),
            pltpu.VMEM((2, PAIR, HD), low),
            pltpu.VMEM((2, tokens, HALF), low),
            dma((9,)),
            dma((2, partners)), dma((2, partners)),
            dma((3,)), dma((3,)),
            dma((2, 2)), dma((2, 2)),
            dma((2,)), dma((2,)),
            dma((2, partners)), dma((2, partners)),
            dma((1,)), dma((1,)),
        ],
        compiler_params=pltpu.CompilerParams(
            collective_id=0, has_side_effects=True, vmem_limit_bytes=62 * 2**20
        ),
    )(query, keys, values, grad_out, delta.T, segments.reshape(-1, TOK)))


def solution(mesh):
    return jax.shard_map(
        on_device,
        mesh=mesh,
        in_specs=(
            P("tok", "hd"),
            P(("tok", "hd"), None),
            P(("tok", "hd"), None),
            P("tok", "hd"),
            P("tok", "hd"),
            P(),
        ),
        out_specs=(P("tok", "hd"), P(("tok", "hd"), None), P(("tok", "hd"), None)),
        check_vma=False,
    )
```

```python
import math

import jax
import jax.numpy as jnp
from jax import lax
from jax.experimental import pallas as pl
from jax.experimental.pallas import tpu as pltpu
from jax.sharding import PartitionSpec as P

MESH = pl.DeviceIdType.MESH
HD = 128
HEADS = 8
TOK = 128
PAIR = 2 * TOK
SPAN = 3 * PAIR
SEEN = 5 * TOK
HALF = HEADS * HD
PIECE = 32
FILL = -1e30
SCALE = 1.0 / math.sqrt(HD)
LOG2E = math.log2(math.e)
PARTNERS = [(0, 2), (1, 2), (0, 1), (0, 3), (1, 1), (1, 3), (1, 0)]
NT = (((1,), (1,)), ((), ()))


def aligned(index, size):
    return pl.multiple_of(index * size, size)


def kernel(
    query, keys, values, grad_out, delta, segments,
    dq_out, dkv_out,
    stage, qb, gb, dt, sb, kv, kt, scores, gweights, probs, dscores, bias,
    own, outbox, inbox, totals, dqs,
    local_sem, kv_send, kv_recv, pair_send, pair_recv,
    shift_send, shift_recv, back_send, back_recv, fin_send, fin_recv, dq_send, dq_recv,
):
    tok, hd = lax.axis_index("tok"), lax.axis_index("hd")
    chips = lax.axis_size("tok") // 2
    rows_y = lax.axis_size("hd")
    core, chip = lax.rem(tok, 2), lax.div(tok, 2)
    other = 1 - core

    def local(index, src, dst):
        copy = pltpu.make_async_copy(src, dst, local_sem.at[index])
        copy.start()
        return copy

    def remote(src, dst, send, recv, to_tok, to_hd):
        return pltpu.make_async_remote_copy(
            src_ref=src, dst_ref=dst, send_sem=send, recv_sem=recv,
            device_id=(to_tok, to_hd), device_id_type=MESH,
        )

    def partner(k):
        cross, step = PARTNERS[k]
        pcore = other if cross else core
        return pcore, lax.rem(hd + step, rows_y)

    mine = pl.ds(aligned(2 * hd + core, HD), HD)
    slot = pl.ds(pl.multiple_of((4 + core) * TOK + PIECE * hd, PIECE), PIECE)
    half = pl.ds(aligned(core, HALF), HALF)
    far_half = pl.ds(aligned(other, HALF), HALF)
    my_rows = pl.ds(aligned(core, TOK), TOK)
    loc_stage = [local(0, keys, stage.at[0]), local(1, values, stage.at[1])]
    loc_s = local(2, segments, sb)

    barrier = pltpu.get_barrier_semaphore()
    for k in range(len(PARTNERS)):
        pcore, ph = partner(k)
        pl.semaphore_signal(barrier, 1, device_id=(2 * chip + pcore, ph), device_id_type=MESH)
    for step in (1, 2):
        @pl.when(chip + step < chips)
        def _(step=step):
            pl.semaphore_signal(barrier, 1, device_id=(tok + 2 * step, hd), device_id_type=MESH)

        @pl.when(chip >= step)
        def _(step=step):
            pl.semaphore_signal(barrier, 1, device_id=(tok - 2 * step, hd), device_id_type=MESH)

    near = sum(
        jnp.where(c, 1, 0)
        for c in (chip >= 1, chip >= 2, chip + 1 < chips, chip + 2 < chips)
    )
    pl.semaphore_wait(barrier, len(PARTNERS) + near)

    for copy in loc_stage:
        copy.wait()
    kv_copies = []
    for k in range(len(PARTNERS)):
        pcore, ph = partner(k)
        cols = pl.ds(aligned(2 * ph + pcore, HD), HD)
        copy = remote(
            stage.at[:, :, cols], kv.at[:, slot],
            kv_send.at[k], kv_recv.at[k], 2 * chip + pcore, ph,
        )
        copy.start()
        kv_copies.append(copy)
    loc_kv = local(7, stage.at[:, :, mine], kv.at[:, slot])
    pair_copies = []
    for k, (src, dst) in enumerate((
        (query.at[:, far_half], qb.at[my_rows]),
        (grad_out.at[:, far_half], gb.at[my_rows]),
        (delta, dt.at[core]),
    )):
        copy = remote(src, dst, pair_send.at[k], pair_recv.at[k], 2 * chip + other, hd)
        copy.start()
        pair_copies.append(copy)
    loc_q = local(3, query.at[:, half], qb.at[my_rows])
    loc_g = local(4, grad_out.at[:, half], gb.at[my_rows])
    loc_d = local(5, delta, dt.at[core])

    for step in (1, 2):
        @pl.when(chip < step)
        def _(step=step):
            empty = pl.ds((2 - step) * PAIR, PAIR)
            kv[:, empty, :] = jnp.zeros((2, PAIR, HD), kv.dtype)

        @pl.when(chip + step >= chips)
        def _(step=step):
            inbox[step - 1] = jnp.zeros(inbox.shape[1:], inbox.dtype)

    loc_s.wait()

    def ids(shard):
        row = sb[pl.ds(jnp.maximum(shard, 0), 1), :]
        return jnp.where(shard < 0, -1, row)

    shards = [2 * chip - 4 + s for s in range(6)]
    rows = [ids(s) for s in shards]
    tall = [jnp.transpose(jnp.broadcast_to(r, (TOK, TOK))) for r in rows]
    key_at = lax.broadcasted_iota(jnp.int32, (TOK, TOK), 0)
    query_at = lax.broadcasted_iota(jnp.int32, (TOK, TOK), 1)
    for b in range(2):
        for s in range(5):
            allowed = tall[b + s] == rows[4 + b]
            if s == 4:
                allowed = allowed & (key_at <= query_at)
            bias[b, s * TOK : (s + 1) * TOK, :] = jnp.where(allowed, 0.0, FILL)
    nothing = jnp.zeros((TOK, TOK), probs.dtype)
    for head in range(HEADS):
        for ref in (probs, dscores):
            ref[SEEN:SPAN, head * PAIR : head * PAIR + TOK] = nothing
            ref[0:TOK, head * PAIR + TOK : (head + 1) * PAIR] = nothing

    shift = [[[None] * 2 for _ in range(2)] for _ in range(2)]
    loc_kv.wait()
    for copy in kv_copies:
        copy.wait_recv()
    for which in range(2):
        for step in (2, 1):
            copy = remote(
                kv.at[which, pl.ds(2 * PAIR, PAIR)],
                kv.at[which, pl.ds((2 - step) * PAIR, PAIR)],
                shift_send.at[step - 1, which], shift_recv.at[step - 1, which],
                tok + 2 * step, hd,
            )
            shift[step - 1][which] = copy

            @pl.when(chip + step < chips)
            def _(copy=copy):
                copy.start()

    loc_q.wait()
    loc_g.wait()
    loc_d.wait()
    for copy in pair_copies:
        copy.wait_recv()

    def products(block):
        span = slice(block * PAIR, (block + 1) * PAIR)

        def body(head, _):
            cols = pl.ds(aligned(head, HD), HD)
            scores[head, span, :] = lax.dot_general(
                kv[0, span, :], qb[:, cols], NT, preferred_element_type=jnp.float32
            )
            gweights[head, span, :] = lax.dot_general(
                kv[1, span, :], gb[:, cols], NT, preferred_element_type=jnp.float32
            )
            return 0

        lax.fori_loop(0, HEADS, body, 0, unroll=HEADS)
        kt[:, span] = jnp.transpose(kv[0, span, :])

    products(2)
    for step in (1, 2):
        @pl.when(chip >= step)
        def _(step=step):
            for which in range(2):
                shift[step - 1][which].wait_recv()

        products(2 - step)

    def softmax(head, _):
        for b in range(2):
            span = slice(b * TOK, b * TOK + SEEN)
            lanes = slice(b * TOK, (b + 1) * TOK)
            raw = scores[head, span, lanes] + bias[b]
            top = jnp.max(raw, axis=0, keepdims=True)
            grown = jnp.exp2((raw - top) * (SCALE * LOG2E))
            total = jnp.sum(grown, axis=0, keepdims=True)
            weights = grown * (1.0 / total)
            row_delta = dt[b, pl.ds(core * HEADS + head, 1), :]
            grads = weights * (gweights[head, span, lanes] - row_delta)
            cols = pl.ds(pl.multiple_of(head * PAIR + b * TOK, TOK), TOK)
            probs[span, cols] = weights.astype(probs.dtype)
            dscores[span, cols] = grads.astype(dscores.dtype)
        return 0

    lax.fori_loop(0, HEADS, softmax, 0, unroll=HEADS)

    def key_value_grads(block):
        span = slice(block * PAIR, (block + 1) * PAIR)
        dk = jnp.zeros((PAIR, HD), jnp.float32)
        dv = jnp.zeros((PAIR, HD), jnp.float32)
        for head in range(HEADS):
            lanes = slice(head * PAIR, (head + 1) * PAIR)
            cols = slice(head * HD, (head + 1) * HD)
            dk += jnp.dot(dscores[span, lanes], qb[:, cols], preferred_element_type=jnp.float32)
            dv += jnp.dot(probs[span, lanes], gb[:, cols], preferred_element_type=jnp.float32)
        return dk * SCALE, dv

    back = [None, None]
    for step in (2, 1):
        dk, dv = key_value_grads(2 - step)
        outbox[step - 1, 0] = dk.astype(outbox.dtype)
        outbox[step - 1, 1] = dv.astype(outbox.dtype)
        copy = remote(
            outbox.at[step - 1], inbox.at[step - 1],
            back_send.at[step - 1], back_recv.at[step - 1], tok - 2 * step, hd,
        )
        back[step - 1] = copy

        @pl.when(chip >= step)
        def _(copy=copy):
            copy.start()

    dk, dv = key_value_grads(2)
    own[0] = dk
    own[1] = dv

    def query_grads(head, _):
        lanes = pl.ds(aligned(head, PAIR), PAIR)
        turned = jnp.dot(kt[...], dscores[:, lanes], preferred_element_type=jnp.float32)
        turned = turned * SCALE
        cols = pl.ds(aligned(head, HD), HD)
        for b in range(2):
            block = jnp.transpose(turned[:, b * TOK : (b + 1) * TOK])
            dqs[b, :, cols] = block.astype(dqs.dtype)
        return 0

    lax.fori_loop(0, HEADS, query_grads, 0, unroll=HEADS)
    dq_copy = remote(
        dqs.at[other], dq_out.at[:, half], dq_send.at[0], dq_recv.at[0], 2 * chip + other, hd
    )
    dq_copy.start()
    loc_dq = local(6, dqs.at[core], dq_out.at[:, half])

    for step in (1, 2):
        @pl.when(chip + step < chips)
        def _(step=step):
            back[step - 1].wait_recv()

    for which in range(2):
        total = own[which]
        for step in range(2):
            total += inbox[step, which].astype(jnp.float32)
        totals[which] = total.astype(totals.dtype)
    fin_copies = []
    for k in range(len(PARTNERS)):
        pcore, ph = partner(k)
        src_rows = pl.ds(pl.multiple_of(pcore * TOK + PIECE * ph, PIECE), PIECE)
        copy = remote(
            totals.at[:, src_rows], dkv_out.at[:, :, mine],
            fin_send.at[k], fin_recv.at[k], 2 * chip + pcore, ph,
        )
        copy.start()
        fin_copies.append(copy)
    own_rows = pl.ds(pl.multiple_of(core * TOK + PIECE * hd, PIECE), PIECE)
    loc_dkv = local(8, totals.at[:, own_rows], dkv_out.at[:, :, mine])

    for copy in kv_copies + pair_copies:
        copy.wait_send()
    for step in (1, 2):
        @pl.when(chip + step < chips)
        def _(step=step):
            for which in range(2):
                shift[step - 1][which].wait_send()

        @pl.when(chip >= step)
        def _(step=step):
            back[step - 1].wait_send()

    loc_dq.wait()
    loc_dkv.wait()
    dq_copy.wait()
    for copy in fin_copies:
        copy.wait()


def store(dq, dkv, dq_out, dk_out, dv_out, sems):
    copies = [
        pltpu.make_async_copy(src, dst, sems.at[k])
        for k, (src, dst) in enumerate(
            ((dq, dq_out), (dkv.at[0], dk_out), (dkv.at[1], dv_out))
        )
    ]
    for copy in copies:
        copy.start()
    for copy in copies:
        copy.wait()


def on_device(query, keys, values, grad_out, delta, segments):
    low, full = jnp.bfloat16, jnp.float32
    tokens = query.shape[0]
    dma = pltpu.SemaphoreType.DMA
    partners = len(PARTNERS)
    dq, dkv = pl.pallas_call(
        kernel,
        out_shape=(
            pltpu.VMEM(query.shape, low),
            pltpu.VMEM((2,) + keys.shape, low),
        ),
        in_specs=[pl.BlockSpec(memory_space=pl.ANY)] * 6,
        out_specs=[pl.BlockSpec(memory_space=pltpu.VMEM)] * 2,
        scratch_shapes=[
            pltpu.VMEM((2,) + keys.shape, low),
            pltpu.VMEM((PAIR, HALF), low),
            pltpu.VMEM((PAIR, HALF), low),
            pltpu.VMEM((2,) + delta.shape[::-1], full),
            pltpu.VMEM((segments.shape[0] // TOK, TOK), jnp.int32),
            pltpu.VMEM((2, SPAN, HD), low),
            pltpu.VMEM((HD, SPAN), low),
            pltpu.VMEM((HEADS, SPAN, PAIR), full),
            pltpu.VMEM((HEADS, SPAN, PAIR), full),
            pltpu.VMEM((SPAN, HEADS * PAIR), low),
            pltpu.VMEM((SPAN, HEADS * PAIR), low),
            pltpu.VMEM((2, SEEN, TOK), full),
            pltpu.VMEM((2, PAIR, HD), full),
            pltpu.VMEM((2, 2, PAIR, HD), low),
            pltpu.VMEM((2, 2, PAIR, HD), low),
            pltpu.VMEM((2, PAIR, HD), low),
            pltpu.VMEM((2, tokens, HALF), low),
            dma((9,)),
            dma((partners,)), dma((partners,)),
            dma((3,)), dma((3,)),
            dma((2, 2)), dma((2, 2)),
            dma((2,)), dma((2,)),
            dma((partners,)), dma((partners,)),
            dma((1,)), dma((1,)),
        ],
        compiler_params=pltpu.CompilerParams(
            collective_id=0, has_side_effects=True, vmem_limit_bytes=62 * 2**20
        ),
    )(query, keys, values, grad_out, delta.T, segments.reshape(-1, TOK))
    return tuple(pl.pallas_call(
        store,
        out_shape=tuple(jax.ShapeDtypeStruct(a.shape, low) for a in (query, keys, values)),
        in_specs=[pl.BlockSpec(memory_space=pltpu.VMEM)] * 2,
        out_specs=[pl.BlockSpec(memory_space=pl.ANY)] * 3,
        scratch_shapes=[dma((3,))],
    )(*(pltpu.with_memory_space_constraint(a, pltpu.VMEM) for a in (dq, dkv))))


def solution(mesh):
    return jax.shard_map(
        on_device,
        mesh=mesh,
        in_specs=(
            P("tok", "hd"),
            P(("tok", "hd"), None),
            P(("tok", "hd"), None),
            P("tok", "hd"),
            P("tok", "hd"),
            P(),
        ),
        out_specs=(P("tok", "hd"), P(("tok", "hd"), None), P(("tok", "hd"), None)),
        check_vma=False,
    )
```

```python
import math

import jax
import jax.numpy as jnp
from jax import lax
from jax.experimental import pallas as pl
from jax.experimental.pallas import tpu as pltpu
from jax.sharding import PartitionSpec as P

MESH = pl.DeviceIdType.MESH
HD = 128
HEADS = 8
TOK = 128
PAIR = 2 * TOK
SPAN = 3 * PAIR
SEEN = 5 * TOK
HALF = HEADS * HD
PIECE = 32
FILL = -1e30
SCALE = 1.0 / math.sqrt(HD)
LOG2E = math.log2(math.e)
PARTNERS = [(0, 2), (1, 2), (0, 1), (0, 3), (1, 1), (1, 3), (1, 0)]
NT = (((1,), (1,)), ((), ()))


def aligned(index, size):
    return pl.multiple_of(index * size, size)


def kernel(
    query, keys, values, grad_out, delta, segments,
    dq_out, dkv_out,
    stage, qb, gb, dt, sb, kv, kt, scores, gweights, probs, dscores, bias,
    own, outbox, inbox, totals, dqs,
    local_sem, kv_send, kv_recv, pair_send, pair_recv,
    shift_send, shift_recv, back_send, back_recv, fin_send, fin_recv, dq_send, dq_recv,
):
    tok, hd = lax.axis_index("tok"), lax.axis_index("hd")
    chips = lax.axis_size("tok") // 2
    rows_y = lax.axis_size("hd")
    core, chip = lax.rem(tok, 2), lax.div(tok, 2)
    other = 1 - core

    def local(index, src, dst):
        copy = pltpu.make_async_copy(src, dst, local_sem.at[index])
        copy.start()
        return copy

    def remote(src, dst, send, recv, to_tok, to_hd):
        return pltpu.make_async_remote_copy(
            src_ref=src, dst_ref=dst, send_sem=send, recv_sem=recv,
            device_id=(to_tok, to_hd), device_id_type=MESH,
        )

    def partner(k):
        cross, step = PARTNERS[k]
        pcore = other if cross else core
        return pcore, lax.rem(hd + step, rows_y)

    mine = pl.ds(aligned(2 * hd + core, HD), HD)
    slot = pl.ds(pl.multiple_of((4 + core) * TOK + PIECE * hd, PIECE), PIECE)
    half = pl.ds(aligned(core, HALF), HALF)
    far_half = pl.ds(aligned(other, HALF), HALF)
    my_rows = pl.ds(aligned(core, TOK), TOK)
    loc_stage = [local(0, keys, stage.at[0]), local(1, values, stage.at[1])]
    loc_s = local(2, segments, sb)

    barrier = pltpu.get_barrier_semaphore()
    for k in range(len(PARTNERS)):
        pcore, ph = partner(k)
        pl.semaphore_signal(barrier, 1, device_id=(2 * chip + pcore, ph), device_id_type=MESH)
    for step in (1, 2):
        @pl.when(chip + step < chips)
        def _(step=step):
            pl.semaphore_signal(barrier, 1, device_id=(tok + 2 * step, hd), device_id_type=MESH)

        @pl.when(chip >= step)
        def _(step=step):
            pl.semaphore_signal(barrier, 1, device_id=(tok - 2 * step, hd), device_id_type=MESH)

    near = sum(
        jnp.where(c, 1, 0)
        for c in (chip >= 1, chip >= 2, chip + 1 < chips, chip + 2 < chips)
    )
    pl.semaphore_wait(barrier, len(PARTNERS) + near)

    for copy in loc_stage:
        copy.wait()
    kv_copies = [[], []]
    loc_kv = []
    for which in range(2):
        for k in range(len(PARTNERS)):
            pcore, ph = partner(k)
            cols = pl.ds(aligned(2 * ph + pcore, HD), HD)
            copy = remote(
                stage.at[which, :, cols], kv.at[which, slot],
                kv_send.at[which, k], kv_recv.at[which, k], 2 * chip + pcore, ph,
            )
            copy.start()
            kv_copies[which].append(copy)
        loc_kv.append(local(7 + which, stage.at[which, :, mine], kv.at[which, slot]))
    pair_copies = []
    for k, (src, dst) in enumerate((
        (query.at[:, far_half], qb.at[my_rows]),
        (grad_out.at[:, far_half], gb.at[my_rows]),
        (delta, dt.at[core]),
    )):
        copy = remote(src, dst, pair_send.at[k], pair_recv.at[k], 2 * chip + other, hd)
        copy.start()
        pair_copies.append(copy)
    loc_q = local(3, query.at[:, half], qb.at[my_rows])
    loc_g = local(4, grad_out.at[:, half], gb.at[my_rows])
    loc_d = local(5, delta, dt.at[core])

    for step in (1, 2):
        @pl.when(chip < step)
        def _(step=step):
            empty = pl.ds((2 - step) * PAIR, PAIR)
            kv[:, empty, :] = jnp.zeros((2, PAIR, HD), kv.dtype)

        @pl.when(chip + step >= chips)
        def _(step=step):
            inbox[step - 1] = jnp.zeros(inbox.shape[1:], inbox.dtype)

    loc_s.wait()

    def ids(shard):
        row = sb[pl.ds(jnp.maximum(shard, 0), 1), :]
        return jnp.where(shard < 0, -1, row)

    shards = [2 * chip - 4 + s for s in range(6)]
    rows = [ids(s) for s in shards]
    tall = [jnp.transpose(jnp.broadcast_to(r, (TOK, TOK))) for r in rows]
    key_at = lax.broadcasted_iota(jnp.int32, (TOK, TOK), 0)
    query_at = lax.broadcasted_iota(jnp.int32, (TOK, TOK), 1)
    for b in range(2):
        for s in range(5):
            allowed = tall[b + s] == rows[4 + b]
            if s == 4:
                allowed = allowed & (key_at <= query_at)
            bias[b, s * TOK : (s + 1) * TOK, :] = jnp.where(allowed, 0.0, FILL)
    nothing = jnp.zeros((TOK, TOK), probs.dtype)
    for head in range(HEADS):
        for ref in (probs, dscores):
            ref[SEEN:SPAN, head * PAIR : head * PAIR + TOK] = nothing
            ref[0:TOK, head * PAIR + TOK : (head + 1) * PAIR] = nothing

    shift = [[None] * 2, [None] * 2]
    for which in range(2):
        loc_kv[which].wait()
        for copy in kv_copies[which]:
            copy.wait_recv()
        for step in (2, 1):
            copy = remote(
                kv.at[which, pl.ds(2 * PAIR, PAIR)],
                kv.at[which, pl.ds((2 - step) * PAIR, PAIR)],
                shift_send.at[step - 1, which], shift_recv.at[step - 1, which],
                tok + 2 * step, hd,
            )
            shift[which][step - 1] = copy

            @pl.when(chip + step < chips)
            def _(copy=copy):
                copy.start()

    loc_q.wait()
    loc_g.wait()
    loc_d.wait()
    for copy in pair_copies:
        copy.wait_recv()

    def over_heads(body):
        def step(head, _):
            body(head)
            return 0

        lax.fori_loop(0, HEADS, step, 0, unroll=HEADS)

    def products(which, block):
        span = slice(block * PAIR, (block + 1) * PAIR)
        rows_of, result = ((qb, scores), (gb, gweights))[which]

        def body(head):
            cols = pl.ds(aligned(head, HD), HD)
            result[head, span, :] = lax.dot_general(
                kv[which, span, :], rows_of[:, cols], NT, preferred_element_type=jnp.float32
            )

        over_heads(body)

    def arrival(which, step):
        @pl.when(chip >= step)
        def _():
            shift[which][step - 1].wait_recv()

    def parts(head, b):
        span = slice(b * TOK, b * TOK + SEEN)
        lanes = slice(b * TOK, (b + 1) * TOK)
        cols = pl.ds(pl.multiple_of(head * PAIR + b * TOK, TOK), TOK)
        return span, lanes, cols

    def softmax(head):
        for b in range(2):
            span, lanes, cols = parts(head, b)
            raw = scores[head, span, lanes] + bias[b]
            top = jnp.max(raw, axis=0, keepdims=True)
            grown = jnp.exp2((raw - top) * (SCALE * LOG2E))
            total = jnp.sum(grown, axis=0, keepdims=True)
            weights = grown * (1.0 / total)
            scores[head, span, lanes] = weights
            probs[span, cols] = weights.astype(probs.dtype)

    def score_grads(head):
        for b in range(2):
            span, lanes, cols = parts(head, b)
            row_delta = dt[b, pl.ds(core * HEADS + head, 1), :]
            grads = scores[head, span, lanes] * (gweights[head, span, lanes] - row_delta)
            dscores[span, cols] = grads.astype(dscores.dtype)

    def grads_of(which, block):
        span = slice(block * PAIR, (block + 1) * PAIR)
        terms, rows_of = ((dscores, qb), (probs, gb))[which]
        total = jnp.zeros((PAIR, HD), jnp.float32)
        for head in range(HEADS):
            total += jnp.dot(
                terms[span, head * PAIR : (head + 1) * PAIR],
                rows_of[:, head * HD : (head + 1) * HD],
                preferred_element_type=jnp.float32,
            )
        return total if which else total * SCALE

    def send_back(which):
        for step in (2, 1):
            outbox[step - 1, which] = grads_of(which, 2 - step).astype(outbox.dtype)
            copy = remote(
                outbox.at[step - 1, which], inbox.at[step - 1, which],
                back_send.at[step - 1, which], back_recv.at[step - 1, which],
                tok - 2 * step, hd,
            )
            back[which][step - 1] = copy

            @pl.when(chip >= step)
            def _(copy=copy):
                copy.start()

        own[which] = grads_of(which, 2)

    back = [[None] * 2, [None] * 2]
    products(0, 2)
    products(1, 2)
    for step in (1, 2):
        arrival(0, step)
        products(0, 2 - step)
    over_heads(softmax)
    send_back(1)
    for step in (1, 2):
        arrival(1, step)
        products(1, 2 - step)
    over_heads(score_grads)
    send_back(0)

    for block in range(3):
        span = slice(block * PAIR, (block + 1) * PAIR)
        kt[:, span] = jnp.transpose(kv[0, span, :])

    def query_grads(head):
        lanes = pl.ds(aligned(head, PAIR), PAIR)
        turned = jnp.dot(kt[...], dscores[:, lanes], preferred_element_type=jnp.float32)
        turned = turned * SCALE
        cols = pl.ds(aligned(head, HD), HD)
        for b in range(2):
            block = jnp.transpose(turned[:, b * TOK : (b + 1) * TOK])
            dqs[b, :, cols] = block.astype(dqs.dtype)

    over_heads(query_grads)
    dq_copy = remote(
        dqs.at[other], dq_out.at[:, half], dq_send.at[0], dq_recv.at[0], 2 * chip + other, hd
    )
    dq_copy.start()
    loc_dq = local(6, dqs.at[core], dq_out.at[:, half])

    own_rows = pl.ds(pl.multiple_of(core * TOK + PIECE * hd, PIECE), PIECE)
    fin_copies = []
    loc_out = []
    for which in (1, 0):
        for step in (1, 2):
            @pl.when(chip + step < chips)
            def _(step=step, which=which):
                back[which][step - 1].wait_recv()

        total = own[which]
        for step in range(2):
            total += inbox[step, which].astype(jnp.float32)
        totals[which] = total.astype(totals.dtype)
        for k in range(len(PARTNERS)):
            pcore, ph = partner(k)
            src_rows = pl.ds(pl.multiple_of(pcore * TOK + PIECE * ph, PIECE), PIECE)
            copy = remote(
                totals.at[which, src_rows], dkv_out.at[which, :, mine],
                fin_send.at[which, k], fin_recv.at[which, k], 2 * chip + pcore, ph,
            )
            copy.start()
            fin_copies.append(copy)
        loc_out.append(local(9 + which, totals.at[which, own_rows], dkv_out.at[which, :, mine]))

    for copy in kv_copies[0] + kv_copies[1] + pair_copies:
        copy.wait_send()
    for step in (1, 2):
        @pl.when(chip + step < chips)
        def _(step=step):
            for which in range(2):
                shift[which][step - 1].wait_send()

        @pl.when(chip >= step)
        def _(step=step):
            for which in range(2):
                back[which][step - 1].wait_send()

    loc_dq.wait()
    for copy in loc_out:
        copy.wait()
    dq_copy.wait()
    for copy in fin_copies:
        copy.wait()


def store(dq, dkv, dq_out, dk_out, dv_out, sems):
    copies = [
        pltpu.make_async_copy(src, dst, sems.at[k])
        for k, (src, dst) in enumerate(
            ((dq, dq_out), (dkv.at[0], dk_out), (dkv.at[1], dv_out))
        )
    ]
    for copy in copies:
        copy.start()
    for copy in copies:
        copy.wait()


def on_device(query, keys, values, grad_out, delta, segments):
    low, full = jnp.bfloat16, jnp.float32
    tokens = query.shape[0]
    dma = pltpu.SemaphoreType.DMA
    partners = len(PARTNERS)
    dq, dkv = pl.pallas_call(
        kernel,
        out_shape=(
            pltpu.VMEM(query.shape, low),
            pltpu.VMEM((2,) + keys.shape, low),
        ),
        in_specs=[pl.BlockSpec(memory_space=pl.ANY)] * 6,
        out_specs=[pl.BlockSpec(memory_space=pltpu.VMEM)] * 2,
        scratch_shapes=[
            pltpu.VMEM((2,) + keys.shape, low),
            pltpu.VMEM((PAIR, HALF), low),
            pltpu.VMEM((PAIR, HALF), low),
            pltpu.VMEM((2,) + delta.shape[::-1], full),
            pltpu.VMEM((segments.shape[0] // TOK, TOK), jnp.int32),
            pltpu.VMEM((2, SPAN, HD), low),
            pltpu.VMEM((HD, SPAN), low),
            pltpu.VMEM((HEADS, SPAN, PAIR), full),
            pltpu.VMEM((HEADS, SPAN, PAIR), full),
            pltpu.VMEM((SPAN, HEADS * PAIR), low),
            pltpu.VMEM((SPAN, HEADS * PAIR), low),
            pltpu.VMEM((2, SEEN, TOK), full),
            pltpu.VMEM((2, PAIR, HD), full),
            pltpu.VMEM((2, 2, PAIR, HD), low),
            pltpu.VMEM((2, 2, PAIR, HD), low),
            pltpu.VMEM((2, PAIR, HD), low),
            pltpu.VMEM((2, tokens, HALF), low),
            dma((11,)),
            dma((2, partners)), dma((2, partners)),
            dma((3,)), dma((3,)),
            dma((2, 2)), dma((2, 2)),
            dma((2, 2)), dma((2, 2)),
            dma((2, partners)), dma((2, partners)),
            dma((1,)), dma((1,)),
        ],
        compiler_params=pltpu.CompilerParams(
            collective_id=0, has_side_effects=True, vmem_limit_bytes=62 * 2**20
        ),
    )(query, keys, values, grad_out, delta.T, segments.reshape(-1, TOK))
    return tuple(pl.pallas_call(
        store,
        out_shape=tuple(jax.ShapeDtypeStruct(a.shape, low) for a in (query, keys, values)),
        in_specs=[pl.BlockSpec(memory_space=pltpu.VMEM)] * 2,
        out_specs=[pl.BlockSpec(memory_space=pl.ANY)] * 3,
        scratch_shapes=[dma((3,))],
    )(*(pltpu.with_memory_space_constraint(a, pltpu.VMEM) for a in (dq, dkv))))


def solution(mesh):
    return jax.shard_map(
        on_device,
        mesh=mesh,
        in_specs=(
            P("tok", "hd"),
            P(("tok", "hd"), None),
            P(("tok", "hd"), None),
            P("tok", "hd"),
            P("tok", "hd"),
            P(),
        ),
        out_specs=(P("tok", "hd"), P(("tok", "hd"), None), P(("tok", "hd"), None)),
        check_vma=False,
    )
```

```python
import math

import jax
import jax.numpy as jnp
from jax import lax
from jax.experimental import pallas as pl
from jax.experimental.pallas import tpu as pltpu
from jax.sharding import PartitionSpec as P

MESH = pl.DeviceIdType.MESH
HD = 128
HEADS = 8
TOK = 128
PAIR = 2 * TOK
SPAN = 3 * PAIR
SEEN = 5 * TOK
HALF = HEADS * HD
PIECE = 32
FILL = -1e30
SCALE = 1.0 / math.sqrt(HD)
LOG2E = math.log2(math.e)
PLACES = [(0, 2), (1, 2), (0, 1), (0, 3), (1, 1), (1, 3), (1, 0), (0, 0)]
STEPS = (2, 1, 0)
NT = (((1,), (1,)), ((), ()))


def aligned(index, size):
    return pl.multiple_of(index * size, size)


def kernel(
    query, keys, values, grad_out, delta, segments,
    dq_out, dkv_out,
    stage, qb, gb, dt, sb, kv, kt, scores, gweights, probs, dscores, bias, stats,
    terms, gathered, dqs,
    local_sem, kv_send, kv_recv, pair_send, pair_recv,
    back_send, back_recv, dq_send, dq_recv,
):
    tok, hd = lax.axis_index("tok"), lax.axis_index("hd")
    chips = lax.axis_size("tok") // 2
    rows_y = lax.axis_size("hd")
    core, chip = lax.rem(tok, 2), lax.div(tok, 2)
    other = 1 - core

    def local(index, src, dst):
        copy = pltpu.make_async_copy(src, dst, local_sem.at[index])
        copy.start()
        return copy

    def remote(src, dst, send, recv, to_tok, to_hd):
        return pltpu.make_async_remote_copy(
            src_ref=src, dst_ref=dst, send_sem=send, recv_sem=recv,
            device_id=(to_tok, to_hd), device_id_type=MESH,
        )

    def place(k):
        cross, step = PLACES[k]
        pcore = other if cross else core
        return pcore, lax.rem(hd + step, rows_y)

    def places(step):
        return range(len(PLACES) if step else len(PLACES) - 1)

    def only_if(step, condition, action):
        if step:
            pl.when(condition)(action)
        else:
            action()

    mine = pl.ds(aligned(2 * hd + core, HD), HD)
    half = pl.ds(aligned(core, HALF), HALF)
    far_half = pl.ds(aligned(other, HALF), HALF)
    my_rows = pl.ds(aligned(core, TOK), TOK)
    loc_stage = [local(0, keys, stage.at[0]), local(1, values, stage.at[1])]
    loc_s = local(2, segments, sb)

    barrier = pltpu.get_barrier_semaphore()
    for step in STEPS:
        for ahead in (1, -1) if step else (1,):
            def greet(step=step, ahead=ahead):
                for k in places(step):
                    pcore, ph = place(k)
                    pl.semaphore_signal(
                        barrier, 1, device_id=(2 * (chip + ahead * step) + pcore, ph),
                        device_id_type=MESH,
                    )

            only_if(step, chip + step < chips if ahead > 0 else chip >= step, greet)

    near = sum(
        jnp.where(c, 1, 0)
        for c in (chip >= 1, chip >= 2, chip + 1 < chips, chip + 2 < chips)
    )
    pl.semaphore_wait(barrier, len(PLACES) - 1 + len(PLACES) * near)

    for copy in loc_stage:
        copy.wait()
    kv_copies = [[[] for _ in range(3)] for _ in range(2)]
    loc_kv = []

    def send_rows(which):
        for step in STEPS:
            slot = pl.ds(
                pl.multiple_of((4 - 2 * step + core) * TOK + PIECE * hd, PIECE), PIECE
            )
            for k in places(step):
                pcore, ph = place(k)
                cols = pl.ds(aligned(2 * ph + pcore, HD), HD)
                kv_copies[which][step].append(remote(
                    stage.at[which, :, cols], kv.at[which, slot],
                    kv_send.at[which, step, k], kv_recv.at[which, step, k],
                    2 * (chip + step) + pcore, ph,
                ))

            def start(step=step):
                for copy in kv_copies[which][step]:
                    copy.start()

            only_if(step, chip + step < chips, start)
        loc_kv.append(local(7 + which, stage.at[which, :, mine], kv.at[which, slot]))

    pair_copies = []

    def to_other_core(src, dst):
        k = len(pair_copies)
        copy = remote(src, dst, pair_send.at[k], pair_recv.at[k], 2 * chip + other, hd)
        copy.start()
        pair_copies.append(copy)

    send_rows(0)
    to_other_core(query.at[:, far_half], qb.at[my_rows])
    loc_q = local(3, query.at[:, half], qb.at[my_rows])
    send_rows(1)
    to_other_core(grad_out.at[:, far_half], gb.at[my_rows])
    to_other_core(delta, dt.at[core])
    loc_g = local(4, grad_out.at[:, half], gb.at[my_rows])
    loc_d = local(5, delta, dt.at[core])

    for step in (1, 2):
        @pl.when(chip < step)
        def _(step=step):
            empty = pl.ds((2 - step) * PAIR, PAIR)
            kv[:, empty, :] = jnp.zeros((2, PAIR, HD), kv.dtype)

        @pl.when(chip + step >= chips)
        def _(step=step):
            for which in range(2):
                gathered[which, step] = jnp.zeros(gathered.shape[2:], gathered.dtype)

    loc_s.wait()

    def ids(shard):
        row = sb[pl.ds(jnp.maximum(shard, 0), 1), :]
        return jnp.where(shard < 0, -1, row)

    shards = [2 * chip - 4 + s for s in range(6)]
    rows = [ids(s) for s in shards]
    tall = [jnp.transpose(jnp.broadcast_to(r, (TOK, TOK))) for r in rows]
    key_at = lax.broadcasted_iota(jnp.int32, (TOK, TOK), 0)
    query_at = lax.broadcasted_iota(jnp.int32, (TOK, TOK), 1)
    for b in range(2):
        for s in range(5):
            allowed = tall[b + s] == rows[4 + b]
            if s == 4:
                allowed = allowed & (key_at <= query_at)
            bias[b, s * TOK : (s + 1) * TOK, :] = jnp.where(allowed, 0.0, FILL)
    nothing = jnp.zeros((TOK, TOK), probs.dtype)
    for head in range(HEADS):
        for ref in (probs, dscores):
            ref[SEEN:SPAN, head * PAIR : head * PAIR + TOK] = nothing
            ref[0:TOK, head * PAIR + TOK : (head + 1) * PAIR] = nothing

    loc_q.wait()
    loc_g.wait()
    loc_d.wait()
    for copy in pair_copies:
        copy.wait_recv()

    def over_heads(body):
        def step(head, _):
            body(head)
            return 0

        lax.fori_loop(0, HEADS, step, 0, unroll=HEADS)

    def products(which, block):
        span = slice(block * PAIR, (block + 1) * PAIR)
        rows_of, result = ((qb, scores), (gb, gweights))[which]

        def body(head):
            cols = pl.ds(aligned(head, HD), HD)
            result[head, span, :] = lax.dot_general(
                kv[which, span, :], rows_of[:, cols], NT, preferred_element_type=jnp.float32
            )

        over_heads(body)

    def arrival(which, step):
        def wait():
            for copy in kv_copies[which][step]:
                copy.wait_recv()
            if not step:
                loc_kv[which].wait()

        only_if(step, chip >= step, wait)

    def lanes_of(head, b):
        lanes = slice(b * TOK, (b + 1) * TOK)
        cols = pl.ds(pl.multiple_of(head * PAIR + b * TOK, TOK), TOK)
        return lanes, cols

    def near_part(head):
        for b in range(2):
            span = slice(PAIR, b * TOK + SEEN)
            lanes, _ = lanes_of(head, b)
            raw = scores[head, span, lanes] + bias[b, PAIR - b * TOK : SEEN, :]
            top = jnp.max(raw, axis=0, keepdims=True)
            grown = jnp.exp2((raw - top) * (SCALE * LOG2E))
            scores[head, span, lanes] = grown
            stats[0, b, pl.ds(head, 1), :] = top
            stats[1, b, pl.ds(head, 1), :] = jnp.sum(grown, axis=0, keepdims=True)

    def far_part(head):
        for b in range(2):
            span = slice(b * TOK, PAIR)
            lanes, cols = lanes_of(head, b)
            raw = scores[head, span, lanes] + bias[b, 0 : PAIR - b * TOK, :]
            near_top = stats[0, b, pl.ds(head, 1), :]
            near_total = stats[1, b, pl.ds(head, 1), :]
            top = jnp.maximum(near_top, jnp.max(raw, axis=0, keepdims=True))
            grown = jnp.exp2((raw - top) * (SCALE * LOG2E))
            lift = jnp.exp2((near_top - top) * (SCALE * LOG2E))
            total = near_total * lift + jnp.sum(grown, axis=0, keepdims=True)
            share = 1.0 / total
            weights = grown * share
            stats[0, b, pl.ds(head, 1), :] = lift * share
            scores[head, span, lanes] = weights
            probs[span, cols] = weights.astype(probs.dtype)

    def near_weights(head):
        for b in range(2):
            span = slice(PAIR, b * TOK + SEEN)
            lanes, cols = lanes_of(head, b)
            weights = scores[head, span, lanes] * stats[0, b, pl.ds(head, 1), :]
            scores[head, span, lanes] = weights
            probs[span, cols] = weights.astype(probs.dtype)

    def score_grads(head):
        for b in range(2):
            span = slice(b * TOK, b * TOK + SEEN)
            lanes, cols = lanes_of(head, b)
            row_delta = dt[b, pl.ds(core * HEADS + head, 1), :]
            grads = scores[head, span, lanes] * (gweights[head, span, lanes] - row_delta)
            dscores[span, cols] = grads.astype(dscores.dtype)

    def grads_of(which, block):
        span = slice(block * PAIR, (block + 1) * PAIR)
        factors, rows_of = ((dscores, qb), (probs, gb))[which]
        total = jnp.zeros((PAIR, HD), jnp.float32)
        for head in range(HEADS):
            total += jnp.dot(
                factors[span, head * PAIR : (head + 1) * PAIR],
                rows_of[:, head * HD : (head + 1) * HD],
                preferred_element_type=jnp.float32,
            )
        return total if which else total * SCALE

    def rows_at(k):
        pcore, ph = place(k)
        return pl.ds(pl.multiple_of(pcore * TOK + PIECE * ph, PIECE), PIECE)

    back = [[[] for _ in range(3)] for _ in range(2)]
    loc_back = [None] * 2

    def send_back(which, step):
        terms[which, step] = grads_of(which, 2 - step).astype(terms.dtype)
        for k in places(step):
            pcore, ph = place(k)
            back[which][step].append(remote(
                terms.at[which, step, rows_at(k)], gathered.at[which, step, :, mine],
                back_send.at[which, step, k], back_recv.at[which, step, k],
                2 * (chip - step) + pcore, ph,
            ))

        def start():
            for copy in back[which][step]:
                copy.start()

        only_if(step, chip >= step, start)
        if not step:
            own_rows = rows_at(len(PLACES) - 1)
            loc_back[which] = local(
                9 + which, terms.at[which, 0, own_rows], gathered.at[which, 0, :, mine]
            )

    arrival(0, 0)
    products(0, 2)
    arrival(1, 0)
    products(1, 2)
    arrival(0, 1)
    products(0, 1)
    over_heads(near_part)
    arrival(0, 2)
    products(0, 0)
    over_heads(far_part)
    send_back(1, 2)
    over_heads(near_weights)
    send_back(1, 1)
    send_back(1, 0)
    for step in (1, 2):
        arrival(1, step)
        products(1, 2 - step)
    over_heads(score_grads)
    send_back(0, 2)
    send_back(0, 1)
    send_back(0, 0)

    for block in range(3):
        span = slice(block * PAIR, (block + 1) * PAIR)
        kt[:, span] = jnp.transpose(kv[0, span, :])

    def query_grads(head):
        lanes = pl.ds(aligned(head, PAIR), PAIR)
        turned = jnp.dot(kt[...], dscores[:, lanes], preferred_element_type=jnp.float32)
        turned = turned * SCALE
        cols = pl.ds(aligned(head, HD), HD)
        for b in range(2):
            block = jnp.transpose(turned[:, b * TOK : (b + 1) * TOK])
            dqs[b, :, cols] = block.astype(dqs.dtype)

    over_heads(query_grads)
    dq_copy = remote(
        dqs.at[other], dq_out.at[:, half], dq_send.at[0], dq_recv.at[0], 2 * chip + other, hd
    )
    dq_copy.start()
    loc_dq = local(6, dqs.at[core], dq_out.at[:, half])

    for which in (1, 0):
        for step in STEPS:
            def wait(which=which, step=step):
                for copy in back[which][step]:
                    copy.wait_recv()

            only_if(step, chip + step < chips, wait)
        loc_back[which].wait()
        total = gathered[which, 0].astype(jnp.float32)
        for step in (1, 2):
            total += gathered[which, step].astype(jnp.float32)
        dkv_out[which] = total.astype(dkv_out.dtype)

    for copy in pair_copies:
        copy.wait_send()
    for which in range(2):
        for step in STEPS:
            def sent(copies):
                for copy in copies:
                    copy.wait_send()

            only_if(step, chip + step < chips, lambda: sent(kv_copies[which][step]))
            only_if(step, chip >= step, lambda: sent(back[which][step]))
    loc_dq.wait()
    dq_copy.wait()


def store(dq, dkv, dq_out, dk_out, dv_out, sems):
    copies = [
        pltpu.make_async_copy(src, dst, sems.at[k])
        for k, (src, dst) in enumerate(
            ((dq, dq_out), (dkv.at[0], dk_out), (dkv.at[1], dv_out))
        )
    ]
    for copy in copies:
        copy.start()
    for copy in copies:
        copy.wait()


def on_device(query, keys, values, grad_out, delta, segments):
    low, full = jnp.bfloat16, jnp.float32
    tokens = query.shape[0]
    dma = pltpu.SemaphoreType.DMA
    places = len(PLACES)
    dq, dkv = pl.pallas_call(
        kernel,
        out_shape=(
            pltpu.VMEM(query.shape, low),
            pltpu.VMEM((2,) + keys.shape, low),
        ),
        in_specs=[pl.BlockSpec(memory_space=pl.ANY)] * 6,
        out_specs=[pl.BlockSpec(memory_space=pltpu.VMEM)] * 2,
        scratch_shapes=[
            pltpu.VMEM((2,) + keys.shape, low),
            pltpu.VMEM((PAIR, HALF), low),
            pltpu.VMEM((PAIR, HALF), low),
            pltpu.VMEM((2,) + delta.shape[::-1], full),
            pltpu.VMEM((segments.shape[0] // TOK, TOK), jnp.int32),
            pltpu.VMEM((2, SPAN, HD), low),
            pltpu.VMEM((HD, SPAN), low),
            pltpu.VMEM((HEADS, SPAN, PAIR), full),
            pltpu.VMEM((HEADS, SPAN, PAIR), full),
            pltpu.VMEM((SPAN, HEADS * PAIR), low),
            pltpu.VMEM((SPAN, HEADS * PAIR), low),
            pltpu.VMEM((2, SEEN, TOK), full),
            pltpu.VMEM((2, 2, HEADS, TOK), full),
            pltpu.VMEM((2, 3, PAIR, HD), low),
            pltpu.VMEM((2, 3) + keys.shape, low),
            pltpu.VMEM((2, tokens, HALF), low),
            dma((11,)),
            dma((2, 3, places)), dma((2, 3, places)),
            dma((3,)), dma((3,)),
            dma((2, 3, places)), dma((2, 3, places)),
            dma((1,)), dma((1,)),
        ],
        compiler_params=pltpu.CompilerParams(
            collective_id=0, has_side_effects=True, vmem_limit_bytes=62 * 2**20
        ),
    )(query, keys, values, grad_out, delta.T, segments.reshape(-1, TOK))
    return tuple(pl.pallas_call(
        store,
        out_shape=tuple(jax.ShapeDtypeStruct(a.shape, low) for a in (query, keys, values)),
        in_specs=[pl.BlockSpec(memory_space=pltpu.VMEM)] * 2,
        out_specs=[pl.BlockSpec(memory_space=pl.ANY)] * 3,
        scratch_shapes=[dma((3,))],
    )(*(pltpu.with_memory_space_constraint(a, pltpu.VMEM) for a in (dq, dkv))))


def solution(mesh):
    return jax.shard_map(
        on_device,
        mesh=mesh,
        in_specs=(
            P("tok", "hd"),
            P(("tok", "hd"), None),
            P(("tok", "hd"), None),
            P("tok", "hd"),
            P("tok", "hd"),
            P(),
        ),
        out_specs=(P("tok", "hd"), P(("tok", "hd"), None), P(("tok", "hd"), None)),
        check_vma=False,
    )
```

```python
import math

import jax
import jax.numpy as jnp
from jax import lax
from jax.experimental import pallas as pl
from jax.experimental.pallas import tpu as pltpu
from jax.sharding import PartitionSpec as P

MESH = pl.DeviceIdType.MESH
HD = 128
HEADS = 8
TOK = 128
PAIR = 2 * TOK
SPAN = 3 * PAIR
SEEN = 5 * TOK
HALF = HEADS * HD
PIECE = 32
FILL = -1e30
SCALE = 1.0 / math.sqrt(HD)
LOG2E = math.log2(math.e)
PLACES = [(0, 2), (1, 2), (0, 1), (0, 3), (1, 1), (1, 3), (1, 0), (0, 0)]
STEPS = (2, 1, 0)
NT = (((1,), (1,)), ((), ()))


def aligned(index, size):
    return pl.multiple_of(index * size, size)


def kernel(
    query, keys, values, grad_out, delta, segments,
    dq_out, dkv_out,
    stage, qb, gb, dt, sb, kv, kt, scores, gweights, probs, dscores, bias, stats,
    terms, gathered, dqs,
    local_sem, kv_send, kv_recv, pair_send, pair_recv,
    back_send, back_recv, dq_send, dq_recv,
):
    tok, hd = lax.axis_index("tok"), lax.axis_index("hd")
    chips = lax.axis_size("tok") // 2
    rows_y = lax.axis_size("hd")
    core, chip = lax.rem(tok, 2), lax.div(tok, 2)
    other = 1 - core

    def local(index, src, dst):
        copy = pltpu.make_async_copy(src, dst, local_sem.at[index])
        copy.start()
        return copy

    def remote(src, dst, send, recv, to_tok, to_hd):
        return pltpu.make_async_remote_copy(
            src_ref=src, dst_ref=dst, send_sem=send, recv_sem=recv,
            device_id=(to_tok, to_hd), device_id_type=MESH,
        )

    def place(k):
        cross, step = PLACES[k]
        pcore = other if cross else core
        return pcore, lax.rem(hd + step, rows_y)

    def places(step):
        return range(len(PLACES) if step else len(PLACES) - 1)

    def only_if(step, condition, action):
        if step:
            pl.when(condition)(action)
        else:
            action()

    mine = pl.ds(aligned(2 * hd + core, HD), HD)
    half = pl.ds(aligned(core, HALF), HALF)
    far_half = pl.ds(aligned(other, HALF), HALF)
    my_rows = pl.ds(aligned(core, TOK), TOK)
    loc_stage = [local(0, keys, stage.at[0]), local(1, values, stage.at[1])]
    loc_s = local(2, segments, sb)

    barrier = pltpu.get_barrier_semaphore()
    for step in STEPS:
        def greet(step=step):
            for k in places(step):
                pcore, ph = place(k)
                pl.semaphore_signal(
                    barrier, 1, device_id=(2 * (chip - step) + pcore, ph),
                    device_id_type=MESH,
                )

        only_if(step, chip >= step, greet)

    near = sum(jnp.where(c, 1, 0) for c in (chip + 1 < chips, chip + 2 < chips))
    pl.semaphore_wait(barrier, len(PLACES) - 1 + len(PLACES) * near)

    for copy in loc_stage:
        copy.wait()
    kv_copies = [[[] for _ in range(3)] for _ in range(2)]
    loc_kv = []

    def send_rows(which):
        for step in STEPS:
            slot = pl.ds(
                pl.multiple_of((4 - 2 * step + core) * TOK + PIECE * hd, PIECE), PIECE
            )
            for k in places(step):
                pcore, ph = place(k)
                cols = pl.ds(aligned(2 * ph + pcore, HD), HD)
                kv_copies[which][step].append(remote(
                    stage.at[which, :, cols], kv.at[which, slot],
                    kv_send.at[which, step, k], kv_recv.at[which, step, k],
                    2 * (chip + step) + pcore, ph,
                ))

            def start(step=step):
                for copy in kv_copies[which][step]:
                    copy.start()

            only_if(step, chip + step < chips, start)
        loc_kv.append(local(7 + which, stage.at[which, :, mine], kv.at[which, slot]))

    pair_copies = []

    def to_other_core(src, dst):
        k = len(pair_copies)
        copy = remote(src, dst, pair_send.at[k], pair_recv.at[k], 2 * chip + other, hd)
        copy.start()
        pair_copies.append(copy)

    send_rows(0)
    to_other_core(query.at[:, far_half], qb.at[my_rows])
    loc_q = local(3, query.at[:, half], qb.at[my_rows])
    send_rows(1)
    to_other_core(grad_out.at[:, far_half], gb.at[my_rows])
    to_other_core(delta, dt.at[core])
    loc_g = local(4, grad_out.at[:, half], gb.at[my_rows])
    loc_d = local(5, delta, dt.at[core])

    for step in (1, 2):
        @pl.when(chip < step)
        def _(step=step):
            empty = pl.ds((2 - step) * PAIR, PAIR)
            kv[:, empty, :] = jnp.zeros((2, PAIR, HD), kv.dtype)

        @pl.when(chip + step >= chips)
        def _(step=step):
            for which in range(2):
                gathered[which, step] = jnp.zeros(gathered.shape[2:], gathered.dtype)

    loc_s.wait()

    def ids(shard):
        row = sb[pl.ds(jnp.maximum(shard, 0), 1), :]
        return jnp.where(shard < 0, -1, row)

    shards = [2 * chip - 4 + s for s in range(6)]
    rows = [ids(s) for s in shards]
    tall = [jnp.transpose(jnp.broadcast_to(r, (TOK, TOK))) for r in rows]
    key_at = lax.broadcasted_iota(jnp.int32, (TOK, TOK), 0)
    query_at = lax.broadcasted_iota(jnp.int32, (TOK, TOK), 1)
    for b in range(2):
        for s in range(5):
            allowed = tall[b + s] == rows[4 + b]
            if s == 4:
                allowed = allowed & (key_at <= query_at)
            bias[b, s * TOK : (s + 1) * TOK, :] = jnp.where(allowed, 0.0, FILL)
    nothing = jnp.zeros((TOK, TOK), probs.dtype)
    for head in range(HEADS):
        for ref in (probs, dscores):
            ref[SEEN:SPAN, head * PAIR : head * PAIR + TOK] = nothing
            ref[0:TOK, head * PAIR + TOK : (head + 1) * PAIR] = nothing

    loc_q.wait()
    loc_g.wait()
    loc_d.wait()
    for copy in pair_copies:
        copy.wait_recv()

    def over_heads(body):
        def step(head, _):
            body(head)
            return 0

        lax.fori_loop(0, HEADS, step, 0, unroll=HEADS)

    def products(which, block):
        span = slice(block * PAIR, (block + 1) * PAIR)
        rows_of, result = ((qb, scores), (gb, gweights))[which]

        def body(head):
            cols = pl.ds(aligned(head, HD), HD)
            result[head, span, :] = lax.dot_general(
                kv[which, span, :], rows_of[:, cols], NT, preferred_element_type=jnp.float32
            )

        over_heads(body)

    def arrival(which, step):
        def wait():
            for copy in kv_copies[which][step]:
                copy.wait_recv()
            if not step:
                loc_kv[which].wait()

        only_if(step, chip >= step, wait)

    def lanes_of(head, b):
        lanes = slice(b * TOK, (b + 1) * TOK)
        cols = pl.ds(pl.multiple_of(head * PAIR + b * TOK, TOK), TOK)
        return lanes, cols

    def near_part(head):
        for b in range(2):
            span = slice(PAIR, b * TOK + SEEN)
            lanes, _ = lanes_of(head, b)
            raw = scores[head, span, lanes] + bias[b, PAIR - b * TOK : SEEN, :]
            top = jnp.max(raw, axis=0, keepdims=True)
            grown = jnp.exp2((raw - top) * (SCALE * LOG2E))
            scores[head, span, lanes] = grown
            stats[0, b, pl.ds(head, 1), :] = top
            stats[1, b, pl.ds(head, 1), :] = jnp.sum(grown, axis=0, keepdims=True)

    def far_part(head):
        for b in range(2):
            span = slice(b * TOK, PAIR)
            lanes, cols = lanes_of(head, b)
            raw = scores[head, span, lanes] + bias[b, 0 : PAIR - b * TOK, :]
            near_top = stats[0, b, pl.ds(head, 1), :]
            near_total = stats[1, b, pl.ds(head, 1), :]
            top = jnp.maximum(near_top, jnp.max(raw, axis=0, keepdims=True))
            grown = jnp.exp2((raw - top) * (SCALE * LOG2E))
            lift = jnp.exp2((near_top - top) * (SCALE * LOG2E))
            total = near_total * lift + jnp.sum(grown, axis=0, keepdims=True)
            share = 1.0 / total
            weights = grown * share
            stats[0, b, pl.ds(head, 1), :] = lift * share
            scores[head, span, lanes] = weights
            probs[span, cols] = weights.astype(probs.dtype)

    def near_weights(head):
        for b in range(2):
            span = slice(PAIR, b * TOK + SEEN)
            lanes, cols = lanes_of(head, b)
            weights = scores[head, span, lanes] * stats[0, b, pl.ds(head, 1), :]
            scores[head, span, lanes] = weights
            probs[span, cols] = weights.astype(probs.dtype)

    def score_grads(head, far):
        for b in range(2):
            span = slice(b * TOK, PAIR) if far else slice(PAIR, b * TOK + SEEN)
            lanes, cols = lanes_of(head, b)
            row_delta = dt[b, pl.ds(core * HEADS + head, 1), :]
            grads = scores[head, span, lanes] * (gweights[head, span, lanes] - row_delta)
            dscores[span, cols] = grads.astype(dscores.dtype)

    def grads_of(which, block):
        span = slice(block * PAIR, (block + 1) * PAIR)
        factors, rows_of = ((dscores, qb), (probs, gb))[which]
        total = jnp.zeros((PAIR, HD), jnp.float32)
        for head in range(HEADS):
            total += jnp.dot(
                factors[span, head * PAIR : (head + 1) * PAIR],
                rows_of[:, head * HD : (head + 1) * HD],
                preferred_element_type=jnp.float32,
            )
        return total if which else total * SCALE

    def rows_at(k):
        pcore, ph = place(k)
        return pl.ds(pl.multiple_of(pcore * TOK + PIECE * ph, PIECE), PIECE)

    back = [[[] for _ in range(3)] for _ in range(2)]
    loc_back = [None] * 2

    def send_back(which, step):
        terms[which, step] = grads_of(which, 2 - step).astype(terms.dtype)
        for k in places(step):
            pcore, ph = place(k)
            back[which][step].append(remote(
                terms.at[which, step, rows_at(k)], gathered.at[which, step, :, mine],
                back_send.at[which, step, k], back_recv.at[which, step, k],
                2 * (chip - step) + pcore, ph,
            ))

        def start():
            for copy in back[which][step]:
                copy.start()

        only_if(step, chip >= step, start)
        if not step:
            own_rows = rows_at(len(PLACES) - 1)
            loc_back[which] = local(
                9 + which, terms.at[which, 0, own_rows], gathered.at[which, 0, :, mine]
            )

    arrival(0, 0)
    products(0, 2)
    arrival(1, 0)
    products(1, 2)
    arrival(0, 1)
    products(0, 1)
    over_heads(near_part)
    arrival(0, 2)
    products(0, 0)
    over_heads(far_part)
    send_back(1, 2)
    over_heads(near_weights)
    send_back(1, 1)
    for step in (2, 1):
        arrival(1, step)
        products(1, 2 - step)
        over_heads(lambda head: score_grads(head, step == 2))
        send_back(0, step)
    send_back(1, 0)
    send_back(0, 0)

    for block in range(3):
        span = slice(block * PAIR, (block + 1) * PAIR)
        kt[:, span] = jnp.transpose(kv[0, span, :])

    def query_grads(head):
        lanes = pl.ds(aligned(head, PAIR), PAIR)
        turned = jnp.dot(kt[...], dscores[:, lanes], preferred_element_type=jnp.float32)
        turned = turned * SCALE
        cols = pl.ds(aligned(head, HD), HD)
        for b in range(2):
            block = jnp.transpose(turned[:, b * TOK : (b + 1) * TOK])
            dqs[b, :, cols] = block.astype(dqs.dtype)

    over_heads(query_grads)
    dq_copy = remote(
        dqs.at[other], dq_out.at[:, half], dq_send.at[0], dq_recv.at[0], 2 * chip + other, hd
    )
    dq_copy.start()
    loc_dq = local(6, dqs.at[core], dq_out.at[:, half])

    for which in (1, 0):
        for step in STEPS:
            def wait(which=which, step=step):
                for copy in back[which][step]:
                    copy.wait_recv()

            only_if(step, chip + step < chips, wait)
        loc_back[which].wait()
        total = gathered[which, 0].astype(jnp.float32)
        for step in (1, 2):
            total += gathered[which, step].astype(jnp.float32)
        dkv_out[which] = total.astype(dkv_out.dtype)

    for copy in pair_copies:
        copy.wait_send()
    for which in range(2):
        for step in STEPS:
            def sent(copies):
                for copy in copies:
                    copy.wait_send()

            only_if(step, chip + step < chips, lambda: sent(kv_copies[which][step]))
            only_if(step, chip >= step, lambda: sent(back[which][step]))
    loc_dq.wait()
    dq_copy.wait()


def store(dq, dkv, dq_out, dk_out, dv_out, sems):
    copies = [
        pltpu.make_async_copy(src, dst, sems.at[k])
        for k, (src, dst) in enumerate(
            ((dq, dq_out), (dkv.at[0], dk_out), (dkv.at[1], dv_out))
        )
    ]
    for copy in copies:
        copy.start()
    for copy in copies:
        copy.wait()


def on_device(query, keys, values, grad_out, delta, segments):
    low, full = jnp.bfloat16, jnp.float32
    tokens = query.shape[0]
    dma = pltpu.SemaphoreType.DMA
    places = len(PLACES)
    dq, dkv = pl.pallas_call(
        kernel,
        out_shape=(
            pltpu.VMEM(query.shape, low),
            pltpu.VMEM((2,) + keys.shape, low),
        ),
        in_specs=[pl.BlockSpec(memory_space=pl.ANY)] * 6,
        out_specs=[pl.BlockSpec(memory_space=pltpu.VMEM)] * 2,
        scratch_shapes=[
            pltpu.VMEM((2,) + keys.shape, low),
            pltpu.VMEM((PAIR, HALF), low),
            pltpu.VMEM((PAIR, HALF), low),
            pltpu.VMEM((2,) + delta.shape[::-1], full),
            pltpu.VMEM((segments.shape[0] // TOK, TOK), jnp.int32),
            pltpu.VMEM((2, SPAN, HD), low),
            pltpu.VMEM((HD, SPAN), low),
            pltpu.VMEM((HEADS, SPAN, PAIR), full),
            pltpu.VMEM((HEADS, SPAN, PAIR), full),
            pltpu.VMEM((SPAN, HEADS * PAIR), low),
            pltpu.VMEM((SPAN, HEADS * PAIR), low),
            pltpu.VMEM((2, SEEN, TOK), full),
            pltpu.VMEM((2, 2, HEADS, TOK), full),
            pltpu.VMEM((2, 3, PAIR, HD), low),
            pltpu.VMEM((2, 3) + keys.shape, low),
            pltpu.VMEM((2, tokens, HALF), low),
            dma((11,)),
            dma((2, 3, places)), dma((2, 3, places)),
            dma((3,)), dma((3,)),
            dma((2, 3, places)), dma((2, 3, places)),
            dma((1,)), dma((1,)),
        ],
        compiler_params=pltpu.CompilerParams(
            collective_id=0, has_side_effects=True, vmem_limit_bytes=62 * 2**20
        ),
    )(query, keys, values, grad_out, delta.T, segments.reshape(-1, TOK))
    return tuple(pl.pallas_call(
        store,
        out_shape=tuple(jax.ShapeDtypeStruct(a.shape, low) for a in (query, keys, values)),
        in_specs=[pl.BlockSpec(memory_space=pltpu.VMEM)] * 2,
        out_specs=[pl.BlockSpec(memory_space=pl.ANY)] * 3,
        scratch_shapes=[dma((3,))],
    )(*(pltpu.with_memory_space_constraint(a, pltpu.VMEM) for a in (dq, dkv))))


def solution(mesh):
    return jax.shard_map(
        on_device,
        mesh=mesh,
        in_specs=(
            P("tok", "hd"),
            P(("tok", "hd"), None),
            P(("tok", "hd"), None),
            P("tok", "hd"),
            P("tok", "hd"),
            P(),
        ),
        out_specs=(P("tok", "hd"), P(("tok", "hd"), None), P(("tok", "hd"), None)),
        check_vma=False,
    )
```

```python
import math

import jax
import jax.numpy as jnp
from jax import lax
from jax.experimental import pallas as pl
from jax.experimental.pallas import tpu as pltpu
from jax.sharding import PartitionSpec as P

MESH = pl.DeviceIdType.MESH
HD = 128
HEADS = 8
TOK = 128
PAIR = 2 * TOK
SPAN = 3 * PAIR
SEEN = 5 * TOK
HALF = HEADS * HD
PIECE = 32
FILL = -1e30
SCALE = 1.0 / math.sqrt(HD)
LOG2E = math.log2(math.e)
PLACES = [(0, 2), (1, 2), (0, 1), (0, 3), (1, 1), (1, 3), (1, 0), (0, 0)]
STEPS = (2, 1, 0)
NT = (((1,), (1,)), ((), ()))


def aligned(index, size):
    return pl.multiple_of(index * size, size)


def kernel(
    query, keys, values, grad_out, delta, segments,
    dq_out, dkv_out,
    stage, qb, gb, dt, sb, kv, kt, scores, gweights, probs, dscores, bias, stats,
    terms, gathered, dqs,
    local_sem, kv_send, kv_recv, pair_send, pair_recv,
    back_send, back_recv, dq_send, dq_recv,
):
    tok, hd = lax.axis_index("tok"), lax.axis_index("hd")
    chips = lax.axis_size("tok") // 2
    rows_y = lax.axis_size("hd")
    core, chip = lax.rem(tok, 2), lax.div(tok, 2)
    other = 1 - core

    def local(index, src, dst):
        copy = pltpu.make_async_copy(src, dst, local_sem.at[index])
        copy.start()
        return copy

    def remote(src, dst, send, recv, to_tok, to_hd):
        return pltpu.make_async_remote_copy(
            src_ref=src, dst_ref=dst, send_sem=send, recv_sem=recv,
            device_id=(to_tok, to_hd), device_id_type=MESH,
        )

    def place(k):
        cross, step = PLACES[k]
        pcore = other if cross else core
        return pcore, lax.rem(hd + step, rows_y)

    def places(step):
        return range(len(PLACES) if step else len(PLACES) - 1)

    def only_if(step, condition, action):
        if step:
            pl.when(condition)(action)
        else:
            action()

    mine = pl.ds(aligned(2 * hd + core, HD), HD)
    half = pl.ds(aligned(core, HALF), HALF)
    far_half = pl.ds(aligned(other, HALF), HALF)
    my_rows = pl.ds(aligned(core, TOK), TOK)
    barrier = pltpu.get_barrier_semaphore()
    for step in STEPS:
        def greet(step=step):
            for k in places(step):
                pcore, ph = place(k)
                pl.semaphore_signal(
                    barrier, 1, device_id=(2 * (chip - step) + pcore, ph),
                    device_id_type=MESH,
                )

        only_if(step, chip >= step, greet)

    loc_stage = [local(0, keys, stage.at[0]), local(1, values, stage.at[1])]
    loc_s = local(2, segments, sb)
    near = sum(jnp.where(c, 1, 0) for c in (chip + 1 < chips, chip + 2 < chips))
    pl.semaphore_wait(barrier, len(PLACES) - 1 + len(PLACES) * near)

    for copy in loc_stage:
        copy.wait()
    kv_copies = [[[] for _ in range(3)] for _ in range(2)]

    def send_rows(which):
        for step in STEPS:
            slot = pl.ds(
                pl.multiple_of((4 - 2 * step + core) * TOK + PIECE * hd, PIECE), PIECE
            )
            for k in places(step):
                pcore, ph = place(k)
                cols = pl.ds(aligned(2 * ph + pcore, HD), HD)
                kv_copies[which][step].append(remote(
                    stage.at[which, :, cols], kv.at[which, slot],
                    kv_send.at[which, step], kv_recv.at[which, step],
                    2 * (chip + step) + pcore, ph,
                ))

            def start(step=step):
                for copy in kv_copies[which][step]:
                    copy.start()

            only_if(step, chip + step < chips, start)
        pltpu.make_async_copy(
            stage.at[which, :, mine], kv.at[which, slot], kv_recv.at[which, 0]
        ).start()

    pair_copies = []

    def to_other_core(src, dst):
        k = len(pair_copies)
        copy = remote(src, dst, pair_send.at[k], pair_recv.at[k], 2 * chip + other, hd)
        copy.start()
        pair_copies.append(copy)

    send_rows(0)
    to_other_core(query.at[:, far_half], qb.at[my_rows])
    loc_q = local(3, query.at[:, half], qb.at[my_rows])
    send_rows(1)
    to_other_core(grad_out.at[:, far_half], gb.at[my_rows])
    to_other_core(delta, dt.at[core])
    loc_g = local(4, grad_out.at[:, half], gb.at[my_rows])
    loc_d = local(5, delta, dt.at[core])

    for step in (1, 2):
        @pl.when(chip < step)
        def _(step=step):
            empty = pl.ds((2 - step) * PAIR, PAIR)
            kv[:, empty, :] = jnp.zeros((2, PAIR, HD), kv.dtype)

        @pl.when(chip + step >= chips)
        def _(step=step):
            for which in range(2):
                gathered[which, step] = jnp.zeros(gathered.shape[2:], gathered.dtype)

    loc_s.wait()

    def ids(shard):
        row = sb[pl.ds(jnp.maximum(shard, 0), 1), :]
        return jnp.where(shard < 0, -1, row)

    shards = [2 * chip - 4 + s for s in range(6)]
    rows = [ids(s) for s in shards]
    tall = [jnp.transpose(jnp.broadcast_to(r, (TOK, TOK))) for r in rows]
    key_at = lax.broadcasted_iota(jnp.int32, (TOK, TOK), 0)
    query_at = lax.broadcasted_iota(jnp.int32, (TOK, TOK), 1)
    for b in range(2):
        for s in range(5):
            allowed = tall[b + s] == rows[4 + b]
            if s == 4:
                allowed = allowed & (key_at <= query_at)
            bias[b, s * TOK : (s + 1) * TOK, :] = jnp.where(allowed, 0.0, FILL)
    nothing = jnp.zeros((TOK, TOK), probs.dtype)
    for head in range(HEADS):
        for ref in (probs, dscores):
            ref[SEEN:SPAN, head * PAIR : head * PAIR + TOK] = nothing
            ref[0:TOK, head * PAIR + TOK : (head + 1) * PAIR] = nothing

    loc_q.wait()
    loc_g.wait()
    loc_d.wait()
    for copy in pair_copies:
        copy.wait_recv()

    def over_heads(body):
        def step(head, _):
            body(head)
            return 0

        lax.fori_loop(0, HEADS, step, 0, unroll=HEADS)

    def products(which, block):
        span = slice(block * PAIR, (block + 1) * PAIR)
        rows_of, result = ((qb, scores), (gb, gweights))[which]

        def body(head):
            cols = pl.ds(aligned(head, HD), HD)
            result[head, span, :] = lax.dot_general(
                kv[which, span, :], rows_of[:, cols], NT, preferred_element_type=jnp.float32
            )

        over_heads(body)

    def settle(block, sem):
        pltpu.make_async_copy(block, block, sem).wait()

    def arrival(which, step):
        def wait():
            settle(kv.at[which, pl.ds((2 - step) * PAIR, PAIR)], kv_recv.at[which, step])

        only_if(step, chip >= step, wait)

    def lanes_of(head, b):
        lanes = slice(b * TOK, (b + 1) * TOK)
        cols = pl.ds(pl.multiple_of(head * PAIR + b * TOK, TOK), TOK)
        return lanes, cols

    def near_part(head):
        for b in range(2):
            span = slice(PAIR, b * TOK + SEEN)
            lanes, _ = lanes_of(head, b)
            raw = scores[head, span, lanes] + bias[b, PAIR - b * TOK : SEEN, :]
            top = jnp.max(raw, axis=0, keepdims=True)
            grown = jnp.exp2((raw - top) * (SCALE * LOG2E))
            scores[head, span, lanes] = grown
            stats[0, b, pl.ds(head, 1), :] = top
            stats[1, b, pl.ds(head, 1), :] = jnp.sum(grown, axis=0, keepdims=True)

    def far_part(head):
        for b in range(2):
            span = slice(b * TOK, PAIR)
            lanes, cols = lanes_of(head, b)
            raw = scores[head, span, lanes] + bias[b, 0 : PAIR - b * TOK, :]
            near_top = stats[0, b, pl.ds(head, 1), :]
            near_total = stats[1, b, pl.ds(head, 1), :]
            top = jnp.maximum(near_top, jnp.max(raw, axis=0, keepdims=True))
            grown = jnp.exp2((raw - top) * (SCALE * LOG2E))
            lift = jnp.exp2((near_top - top) * (SCALE * LOG2E))
            total = near_total * lift + jnp.sum(grown, axis=0, keepdims=True)
            share = 1.0 / total
            weights = grown * share
            stats[0, b, pl.ds(head, 1), :] = lift * share
            scores[head, span, lanes] = weights
            probs[span, cols] = weights.astype(probs.dtype)

    def near_weights(head):
        for b in range(2):
            span = slice(PAIR, b * TOK + SEEN)
            lanes, cols = lanes_of(head, b)
            weights = scores[head, span, lanes] * stats[0, b, pl.ds(head, 1), :]
            scores[head, span, lanes] = weights
            probs[span, cols] = weights.astype(probs.dtype)

    def score_grads(head, far):
        for b in range(2):
            span = slice(b * TOK, PAIR) if far else slice(PAIR, b * TOK + SEEN)
            lanes, cols = lanes_of(head, b)
            row_delta = dt[b, pl.ds(core * HEADS + head, 1), :]
            grads = scores[head, span, lanes] * (gweights[head, span, lanes] - row_delta)
            dscores[span, cols] = grads.astype(dscores.dtype)

    def grads_of(which, block):
        span = slice(block * PAIR, (block + 1) * PAIR)
        factors, rows_of = ((dscores, qb), (probs, gb))[which]
        total = jnp.zeros((PAIR, HD), jnp.float32)
        for head in range(HEADS):
            total += jnp.dot(
                factors[span, head * PAIR : (head + 1) * PAIR],
                rows_of[:, head * HD : (head + 1) * HD],
                preferred_element_type=jnp.float32,
            )
        return total if which else total * SCALE

    def rows_at(k):
        pcore, ph = place(k)
        return pl.ds(pl.multiple_of(pcore * TOK + PIECE * ph, PIECE), PIECE)

    back = [[[] for _ in range(3)] for _ in range(2)]

    def send_back(which, step):
        terms[which, step] = grads_of(which, 2 - step).astype(terms.dtype)
        for k in places(step):
            pcore, ph = place(k)
            back[which][step].append(remote(
                terms.at[which, step, rows_at(k)], gathered.at[which, step, :, mine],
                back_send.at[which, step], back_recv.at[which, step],
                2 * (chip - step) + pcore, ph,
            ))

        def start():
            for copy in back[which][step]:
                copy.start()

        only_if(step, chip >= step, start)
        if not step:
            own_rows = rows_at(len(PLACES) - 1)
            pltpu.make_async_copy(
                terms.at[which, 0, own_rows], gathered.at[which, 0, :, mine],
                back_recv.at[which, 0],
            ).start()

    arrival(0, 0)
    products(0, 2)
    arrival(1, 0)
    products(1, 2)
    arrival(0, 1)
    products(0, 1)
    over_heads(near_part)
    arrival(0, 2)
    products(0, 0)
    over_heads(far_part)
    send_back(1, 2)
    over_heads(near_weights)
    send_back(1, 1)
    for step in (2, 1):
        arrival(1, step)
        products(1, 2 - step)
        over_heads(lambda head: score_grads(head, step == 2))
        send_back(0, step)
    send_back(1, 0)
    send_back(0, 0)

    for block in range(3):
        span = slice(block * PAIR, (block + 1) * PAIR)
        kt[:, span] = jnp.transpose(kv[0, span, :])

    def query_grads(head):
        lanes = pl.ds(aligned(head, PAIR), PAIR)
        turned = jnp.dot(kt[...], dscores[:, lanes], preferred_element_type=jnp.float32)
        turned = turned * SCALE
        cols = pl.ds(aligned(head, HD), HD)
        for b in range(2):
            block = jnp.transpose(turned[:, b * TOK : (b + 1) * TOK])
            dqs[b, :, cols] = block.astype(dqs.dtype)

    over_heads(query_grads)
    dq_copy = remote(
        dqs.at[other], dq_out.at[:, half], dq_send.at[0], dq_recv.at[0], 2 * chip + other, hd
    )
    dq_copy.start()
    loc_dq = local(6, dqs.at[core], dq_out.at[:, half])

    for copy in pair_copies:
        copy.wait_send()
    pieces = [pl.ds(0, PIECE * (len(PLACES) - (step == 0))) for step in range(3)]
    for which in (1, 0):
        for step in STEPS:
            def kv_sent():
                settle(kv.at[which, pieces[step]], kv_send.at[which, step])

            def back_sent():
                settle(terms.at[which, step, pieces[step]], back_send.at[which, step])

            def landed():
                settle(gathered.at[which, step], back_recv.at[which, step])

            only_if(step, chip + step < chips, kv_sent)
            only_if(step, chip >= step, back_sent)
            only_if(step, chip + step < chips, landed)
        total = gathered[which, 0].astype(jnp.float32)
        for step in (1, 2):
            total += gathered[which, step].astype(jnp.float32)
        dkv_out[which] = total.astype(dkv_out.dtype)

    loc_dq.wait()
    dq_copy.wait()


def store(dq, dkv, dq_out, dk_out, dv_out, sems):
    copies = [
        pltpu.make_async_copy(src, dst, sems.at[k])
        for k, (src, dst) in enumerate(
            ((dq, dq_out), (dkv.at[0], dk_out), (dkv.at[1], dv_out))
        )
    ]
    for copy in copies:
        copy.start()
    for copy in copies:
        copy.wait()


def on_device(query, keys, values, grad_out, delta, segments):
    low, full = jnp.bfloat16, jnp.float32
    tokens = query.shape[0]
    dma = pltpu.SemaphoreType.DMA
    dq, dkv = pl.pallas_call(
        kernel,
        out_shape=(
            pltpu.VMEM(query.shape, low),
            pltpu.VMEM((2,) + keys.shape, low),
        ),
        in_specs=[pl.BlockSpec(memory_space=pl.ANY)] * 6,
        out_specs=[pl.BlockSpec(memory_space=pltpu.VMEM)] * 2,
        scratch_shapes=[
            pltpu.VMEM((2,) + keys.shape, low),
            pltpu.VMEM((PAIR, HALF), low),
            pltpu.VMEM((PAIR, HALF), low),
            pltpu.VMEM((2,) + delta.shape[::-1], full),
            pltpu.VMEM((segments.shape[0] // TOK, TOK), jnp.int32),
            pltpu.VMEM((2, SPAN, HD), low),
            pltpu.VMEM((HD, SPAN), low),
            pltpu.VMEM((HEADS, SPAN, PAIR), full),
            pltpu.VMEM((HEADS, SPAN, PAIR), full),
            pltpu.VMEM((SPAN, HEADS * PAIR), low),
            pltpu.VMEM((SPAN, HEADS * PAIR), low),
            pltpu.VMEM((2, SEEN, TOK), full),
            pltpu.VMEM((2, 2, HEADS, TOK), full),
            pltpu.VMEM((2, 3, PAIR, HD), low),
            pltpu.VMEM((2, 3) + keys.shape, low),
            pltpu.VMEM((2, tokens, HALF), low),
            dma((11,)),
            dma((2, 3)), dma((2, 3)),
            dma((3,)), dma((3,)),
            dma((2, 3)), dma((2, 3)),
            dma((1,)), dma((1,)),
        ],
        compiler_params=pltpu.CompilerParams(
            collective_id=0, has_side_effects=True, vmem_limit_bytes=62 * 2**20
        ),
    )(query, keys, values, grad_out, delta.T, segments.reshape(-1, TOK))
    return tuple(pl.pallas_call(
        store,
        out_shape=tuple(jax.ShapeDtypeStruct(a.shape, low) for a in (query, keys, values)),
        in_specs=[pl.BlockSpec(memory_space=pltpu.VMEM)] * 2,
        out_specs=[pl.BlockSpec(memory_space=pl.ANY)] * 3,
        scratch_shapes=[dma((3,))],
    )(*(pltpu.with_memory_space_constraint(a, pltpu.VMEM) for a in (dq, dkv))))


def solution(mesh):
    return jax.shard_map(
        on_device,
        mesh=mesh,
        in_specs=(
            P("tok", "hd"),
            P(("tok", "hd"), None),
            P(("tok", "hd"), None),
            P("tok", "hd"),
            P("tok", "hd"),
            P(),
        ),
        out_specs=(P("tok", "hd"), P(("tok", "hd"), None), P(("tok", "hd"), None)),
        check_vma=False,
    )
```

```python
import math

import jax
import jax.numpy as jnp
from jax import lax
from jax.experimental import pallas as pl
from jax.experimental.pallas import tpu as pltpu
from jax.sharding import PartitionSpec as P

MESH = pl.DeviceIdType.MESH
HD = 128
HEADS = 8
TOK = 128
PAIR = 2 * TOK
SPAN = 3 * PAIR
SEEN = 5 * TOK
HALF = HEADS * HD
PIECE = 32
FILL = -1e30
SCALE = 1.0 / math.sqrt(HD)
LOG2E = math.log2(math.e)
PLACES = [(0, 2), (1, 2), (0, 1), (0, 3), (1, 1), (1, 3), (1, 0), (0, 0)]
STEPS = (2, 1, 0)
NT = (((1,), (1,)), ((), ()))


def aligned(index, size):
    return pl.multiple_of(index * size, size)


def kernel(
    query, keys, values, grad_out, delta, segments,
    dq_out, dkv_out,
    stage, qb, gb, dt, sb, kv, kt, scores, gweights, probs, dscores, bias, stats,
    terms, gathered, dqs,
    local_sem, kv_send, kv_recv, pair_send, pair_recv,
    back_send, back_recv, dq_send, dq_recv,
):
    tok, hd = lax.axis_index("tok"), lax.axis_index("hd")
    chips = lax.axis_size("tok") // 2
    rows_y = lax.axis_size("hd")
    core, chip = lax.rem(tok, 2), lax.div(tok, 2)
    other = 1 - core

    def local(index, src, dst):
        copy = pltpu.make_async_copy(src, dst, local_sem.at[index])
        copy.start()
        return copy

    def remote(src, dst, send, recv, to_tok, to_hd):
        return pltpu.make_async_remote_copy(
            src_ref=src, dst_ref=dst, send_sem=send, recv_sem=recv,
            device_id=(to_tok, to_hd), device_id_type=MESH,
        )

    def place(k):
        cross, step = PLACES[k]
        pcore = other if cross else core
        return pcore, lax.rem(hd + step, rows_y)

    def places(step):
        return range(len(PLACES) if step else len(PLACES) - 1)

    def only_if(step, condition, action):
        if step:
            pl.when(condition)(action)
        else:
            action()

    mine = pl.ds(aligned(2 * hd + core, HD), HD)
    half = pl.ds(aligned(core, HALF), HALF)
    far_half = pl.ds(aligned(other, HALF), HALF)
    my_rows = pl.ds(aligned(core, TOK), TOK)
    barrier = pltpu.get_barrier_semaphore()
    for step in STEPS:
        def greet(step=step):
            for k in places(step):
                pcore, ph = place(k)
                pl.semaphore_signal(
                    barrier, 1, device_id=(2 * (chip - step) + pcore, ph),
                    device_id_type=MESH,
                )

        only_if(step, chip >= step, greet)

    loc_stage = [local(0, keys, stage.at[0]), local(1, values, stage.at[1])]
    loc_s = local(2, segments, sb)
    near = sum(jnp.where(c, 1, 0) for c in (chip + 1 < chips, chip + 2 < chips))
    pl.semaphore_wait(barrier, len(PLACES) - 1 + len(PLACES) * near)

    for copy in loc_stage:
        copy.wait()
    kv_copies = [[[] for _ in range(3)] for _ in range(2)]

    def send_rows(which):
        for step in (1, 2, 0):
            slot = pl.ds(
                pl.multiple_of((4 - 2 * step + core) * TOK + PIECE * hd, PIECE), PIECE
            )
            for k in places(step):
                pcore, ph = place(k)
                cols = pl.ds(aligned(2 * ph + pcore, HD), HD)
                kv_copies[which][step].append(remote(
                    stage.at[which, :, cols], kv.at[which, slot],
                    kv_send.at[which, step], kv_recv.at[which, step],
                    2 * (chip + step) + pcore, ph,
                ))

            def start(step=step):
                for copy in kv_copies[which][step]:
                    copy.start()

            only_if(step, chip + step < chips, start)
        pltpu.make_async_copy(
            stage.at[which, :, mine], kv.at[which, slot], kv_recv.at[which, 0]
        ).start()

    pair_copies = []

    def to_other_core(src, dst):
        k = len(pair_copies)
        copy = remote(src, dst, pair_send.at[k], pair_recv.at[k], 2 * chip + other, hd)
        copy.start()
        pair_copies.append(copy)

    send_rows(0)
    to_other_core(query.at[:, far_half], qb.at[my_rows])
    loc_q = local(3, query.at[:, half], qb.at[my_rows])
    send_rows(1)
    to_other_core(grad_out.at[:, far_half], gb.at[my_rows])
    to_other_core(delta, dt.at[core])
    loc_g = local(4, grad_out.at[:, half], gb.at[my_rows])
    loc_d = local(5, delta, dt.at[core])

    for step in (1, 2):
        @pl.when(chip < step)
        def _(step=step):
            empty = pl.ds((2 - step) * PAIR, PAIR)
            kv[:, empty, :] = jnp.zeros((2, PAIR, HD), kv.dtype)

        @pl.when(chip + step >= chips)
        def _(step=step):
            for which in range(2):
                gathered[which, step] = jnp.zeros(gathered.shape[2:], gathered.dtype)

    loc_s.wait()

    def ids(shard):
        row = sb[pl.ds(jnp.maximum(shard, 0), 1), :]
        return jnp.where(shard < 0, -1, row)

    shards = [2 * chip - 4 + s for s in range(6)]
    rows = [ids(s) for s in shards]
    tall = [jnp.transpose(jnp.broadcast_to(r, (TOK, TOK))) for r in rows]
    key_at = lax.broadcasted_iota(jnp.int32, (TOK, TOK), 0)
    query_at = lax.broadcasted_iota(jnp.int32, (TOK, TOK), 1)
    for b in range(2):
        for s in range(5):
            allowed = tall[b + s] == rows[4 + b]
            if s == 4:
                allowed = allowed & (key_at <= query_at)
            bias[b, s * TOK : (s + 1) * TOK, :] = jnp.where(allowed, 0.0, FILL)
    nothing = jnp.zeros((TOK, TOK), probs.dtype)
    for head in range(HEADS):
        for ref in (probs, dscores):
            ref[SEEN:SPAN, head * PAIR : head * PAIR + TOK] = nothing
            ref[0:TOK, head * PAIR + TOK : (head + 1) * PAIR] = nothing

    loc_q.wait()
    loc_g.wait()
    loc_d.wait()
    for copy in pair_copies:
        copy.wait_recv()

    def over_heads(body):
        def step(head, _):
            body(head)
            return 0

        lax.fori_loop(0, HEADS, step, 0, unroll=HEADS)

    def products(which, block):
        span = slice(block * PAIR, (block + 1) * PAIR)
        rows_of, result = ((qb, scores), (gb, gweights))[which]

        def body(head):
            cols = pl.ds(aligned(head, HD), HD)
            result[head, span, :] = lax.dot_general(
                kv[which, span, :], rows_of[:, cols], NT, preferred_element_type=jnp.float32
            )

        over_heads(body)

    def settle(block, sem):
        pltpu.make_async_copy(block, block, sem).wait()

    def arrival(which, step):
        def wait():
            settle(kv.at[which, pl.ds((2 - step) * PAIR, PAIR)], kv_recv.at[which, step])

        only_if(step, chip >= step, wait)

    def lanes_of(head, b):
        lanes = slice(b * TOK, (b + 1) * TOK)
        cols = pl.ds(pl.multiple_of(head * PAIR + b * TOK, TOK), TOK)
        return lanes, cols

    def near_part(head):
        for b in range(2):
            span = slice(PAIR, b * TOK + SEEN)
            lanes, _ = lanes_of(head, b)
            raw = scores[head, span, lanes] + bias[b, PAIR - b * TOK : SEEN, :]
            top = jnp.max(raw, axis=0, keepdims=True)
            grown = jnp.exp2((raw - top) * (SCALE * LOG2E))
            scores[head, span, lanes] = grown
            stats[0, b, pl.ds(head, 1), :] = top
            stats[1, b, pl.ds(head, 1), :] = jnp.sum(grown, axis=0, keepdims=True)

    def far_part(head):
        for b in range(2):
            span = slice(b * TOK, PAIR)
            lanes, cols = lanes_of(head, b)
            raw = scores[head, span, lanes] + bias[b, 0 : PAIR - b * TOK, :]
            near_top = stats[0, b, pl.ds(head, 1), :]
            near_total = stats[1, b, pl.ds(head, 1), :]
            top = jnp.maximum(near_top, jnp.max(raw, axis=0, keepdims=True))
            grown = jnp.exp2((raw - top) * (SCALE * LOG2E))
            lift = jnp.exp2((near_top - top) * (SCALE * LOG2E))
            total = near_total * lift + jnp.sum(grown, axis=0, keepdims=True)
            share = 1.0 / total
            weights = grown * share
            stats[0, b, pl.ds(head, 1), :] = lift * share
            scores[head, span, lanes] = weights
            probs[span, cols] = weights.astype(probs.dtype)

    def near_weights(head):
        for b in range(2):
            span = slice(PAIR, b * TOK + SEEN)
            lanes, cols = lanes_of(head, b)
            weights = scores[head, span, lanes] * stats[0, b, pl.ds(head, 1), :]
            scores[head, span, lanes] = weights
            probs[span, cols] = weights.astype(probs.dtype)

    def score_grads(head, far):
        for b in range(2):
            span = slice(b * TOK, PAIR) if far else slice(PAIR, b * TOK + SEEN)
            lanes, cols = lanes_of(head, b)
            row_delta = dt[b, pl.ds(core * HEADS + head, 1), :]
            grads = scores[head, span, lanes] * (gweights[head, span, lanes] - row_delta)
            dscores[span, cols] = grads.astype(dscores.dtype)

    def grads_of(which, block):
        span = slice(block * PAIR, (block + 1) * PAIR)
        factors, rows_of = ((dscores, qb), (probs, gb))[which]
        total = jnp.zeros((PAIR, HD), jnp.float32)
        for head in range(HEADS):
            total += jnp.dot(
                factors[span, head * PAIR : (head + 1) * PAIR],
                rows_of[:, head * HD : (head + 1) * HD],
                preferred_element_type=jnp.float32,
            )
        return total if which else total * SCALE

    def rows_at(k):
        pcore, ph = place(k)
        return pl.ds(pl.multiple_of(pcore * TOK + PIECE * ph, PIECE), PIECE)

    back = [[[] for _ in range(3)] for _ in range(2)]

    def send_back(which, step):
        terms[which, step] = grads_of(which, 2 - step).astype(terms.dtype)
        for k in places(step):
            pcore, ph = place(k)
            back[which][step].append(remote(
                terms.at[which, step, rows_at(k)], gathered.at[which, step, :, mine],
                back_send.at[which, step], back_recv.at[which, step],
                2 * (chip - step) + pcore, ph,
            ))

        def start():
            for copy in back[which][step]:
                copy.start()

        only_if(step, chip >= step, start)
        if not step:
            own_rows = rows_at(len(PLACES) - 1)
            pltpu.make_async_copy(
                terms.at[which, 0, own_rows], gathered.at[which, 0, :, mine],
                back_recv.at[which, 0],
            ).start()

    arrival(0, 0)
    products(0, 2)
    arrival(1, 0)
    products(1, 2)
    arrival(0, 1)
    products(0, 1)
    over_heads(near_part)
    arrival(0, 2)
    products(0, 0)
    over_heads(far_part)
    send_back(1, 2)
    over_heads(near_weights)
    send_back(1, 1)
    for step in (2, 1):
        arrival(1, step)
        products(1, 2 - step)
        over_heads(lambda head: score_grads(head, step == 2))
        send_back(0, step)
    send_back(1, 0)
    send_back(0, 0)

    for block in range(3):
        span = slice(block * PAIR, (block + 1) * PAIR)
        kt[:, span] = jnp.transpose(kv[0, span, :])

    def query_grads(head):
        lanes = pl.ds(aligned(head, PAIR), PAIR)
        turned = jnp.dot(kt[...], dscores[:, lanes], preferred_element_type=jnp.float32)
        turned = turned * SCALE
        cols = pl.ds(aligned(head, HD), HD)
        for b in range(2):
            block = jnp.transpose(turned[:, b * TOK : (b + 1) * TOK])
            dqs[b, :, cols] = block.astype(dqs.dtype)

    over_heads(query_grads)
    dq_copy = remote(
        dqs.at[other], dq_out.at[:, half], dq_send.at[0], dq_recv.at[0], 2 * chip + other, hd
    )
    dq_copy.start()
    loc_dq = local(6, dqs.at[core], dq_out.at[:, half])

    for copy in pair_copies:
        copy.wait_send()
    pieces = [pl.ds(0, PIECE * (len(PLACES) - (step == 0))) for step in range(3)]
    for which in (1, 0):
        for step in STEPS:
            def kv_sent():
                settle(kv.at[which, pieces[step]], kv_send.at[which, step])

            def back_sent():
                settle(terms.at[which, step, pieces[step]], back_send.at[which, step])

            def landed():
                settle(gathered.at[which, step], back_recv.at[which, step])

            only_if(step, chip + step < chips, kv_sent)
            only_if(step, chip >= step, back_sent)
            only_if(step, chip + step < chips, landed)
        total = gathered[which, 0].astype(jnp.float32)
        for step in (1, 2):
            total += gathered[which, step].astype(jnp.float32)
        dkv_out[which] = total.astype(dkv_out.dtype)

    loc_dq.wait()
    dq_copy.wait()


def store(dq, dkv, dq_out, dk_out, dv_out, sems):
    copies = [
        pltpu.make_async_copy(src, dst, sems.at[k])
        for k, (src, dst) in enumerate(
            ((dq, dq_out), (dkv.at[0], dk_out), (dkv.at[1], dv_out))
        )
    ]
    for copy in copies:
        copy.start()
    for copy in copies:
        copy.wait()


def on_device(query, keys, values, grad_out, delta, segments):
    low, full = jnp.bfloat16, jnp.float32
    tokens = query.shape[0]
    dma = pltpu.SemaphoreType.DMA
    dq, dkv = pl.pallas_call(
        kernel,
        out_shape=(
            pltpu.VMEM(query.shape, low),
            pltpu.VMEM((2,) + keys.shape, low),
        ),
        in_specs=[pl.BlockSpec(memory_space=pl.ANY)] * 6,
        out_specs=[pl.BlockSpec(memory_space=pltpu.VMEM)] * 2,
        scratch_shapes=[
            pltpu.VMEM((2,) + keys.shape, low),
            pltpu.VMEM((PAIR, HALF), low),
            pltpu.VMEM((PAIR, HALF), low),
            pltpu.VMEM((2,) + delta.shape[::-1], full),
            pltpu.VMEM((segments.shape[0] // TOK, TOK), jnp.int32),
            pltpu.VMEM((2, SPAN, HD), low),
            pltpu.VMEM((HD, SPAN), low),
            pltpu.VMEM((HEADS, SPAN, PAIR), full),
            pltpu.VMEM((HEADS, SPAN, PAIR), full),
            pltpu.VMEM((SPAN, HEADS * PAIR), low),
            pltpu.VMEM((SPAN, HEADS * PAIR), low),
            pltpu.VMEM((2, SEEN, TOK), full),
            pltpu.VMEM((2, 2, HEADS, TOK), full),
            pltpu.VMEM((2, 3, PAIR, HD), low),
            pltpu.VMEM((2, 3) + keys.shape, low),
            pltpu.VMEM((2, tokens, HALF), low),
            dma((11,)),
            dma((2, 3)), dma((2, 3)),
            dma((3,)), dma((3,)),
            dma((2, 3)), dma((2, 3)),
            dma((1,)), dma((1,)),
        ],
        compiler_params=pltpu.CompilerParams(
            collective_id=0, has_side_effects=True, vmem_limit_bytes=62 * 2**20
        ),
    )(query, keys, values, grad_out, delta.T, segments.reshape(-1, TOK))
    return tuple(pl.pallas_call(
        store,
        out_shape=tuple(jax.ShapeDtypeStruct(a.shape, low) for a in (query, keys, values)),
        in_specs=[pl.BlockSpec(memory_space=pltpu.VMEM)] * 2,
        out_specs=[pl.BlockSpec(memory_space=pl.ANY)] * 3,
        scratch_shapes=[dma((3,))],
    )(*(pltpu.with_memory_space_constraint(a, pltpu.VMEM) for a in (dq, dkv))))


def solution(mesh):
    return jax.shard_map(
        on_device,
        mesh=mesh,
        in_specs=(
            P("tok", "hd"),
            P(("tok", "hd"), None),
            P(("tok", "hd"), None),
            P("tok", "hd"),
            P("tok", "hd"),
            P(),
        ),
        out_specs=(P("tok", "hd"), P(("tok", "hd"), None), P(("tok", "hd"), None)),
        check_vma=False,
    )
```
